32 devices in a mesh: shots: 2 (over x), gx: 16 (over z, y, core).
Axes of the slice: x: 2, y: 2, z: 4, core: 2. Of those that a mesh axis runs over, the one named last changes fastest.
Arguments:
- forward_field: bfloat16 [512, 2, 8, 4096], P(('shots', 'gx')), parts along dimension 0, may hold values from -3 to 3
- adjoint_field: bfloat16 [512, 2, 8, 4096], P(('shots', 'gx')), parts along dimension 0, may hold values from -3 to 3
Outputs:
- filtered_image: float32 [33, 512, 4096], P(None, ('shots', 'gx')), parts along dimension 1
The draws below stay inside these ranges and needn't reach their ends.
There are 2 independent parts, one for each index of `shots`. The reference program is written for one: setup_inputs(seed, part) draws one part's arguments, and reference() takes and returns one part's arrays. A program takes and returns all parts, laid end to end along the dimension named above; each array names one. Nothing has to cross between parts.
All inputs are finite; a program needn't handle non-finite values.
Results may differ from the reference program's by a relative error of at most 0.0003.
Values may be sent and summed in bfloat16 or wider, within the bound.
No kernel may reach another device: no remote copies, remote signals or barrier semaphores. Data moves between devices by JAX's collectives and lax.ppermute only.
A program may use at most 128 MiB of HBM per device.

```python
import jax
import jax.numpy as jnp
from jax import lax

Y = 64
Z = 64
F = 8
HALF = 16
LAGS = 33
NX = 256


def shard_levels(key, shape, pieces, smallest, high):
    def one(axis_at, parts):
        heights = jax.random.uniform(jax.random.fold_in(jax.random.fold_in(key, 6), axis_at), (parts,), jnp.float32, smallest / len(pieces), high / len(pieces))
        return jnp.repeat(jnp.exp(heights), shape[axis_at] // parts).reshape((-1,) + (1,) * (len(shape) - axis_at - 1))

    gain = one(*pieces[0])
    for cut in pieces[1:]:
        gain = gain * one(*cut)
    return gain


def gaussian(own_key, shape, deviation, limit, pieces=(), kind=jnp.bfloat16):
    level = shard_levels(own_key, shape, pieces, -0.22, 0.18) if pieces else 1.0
    drawn = jax.random.normal(own_key, shape, jnp.float32) * deviation * level
    return jnp.minimum(jnp.maximum(drawn, -limit), limit).astype(kind)


def setup_inputs(seed: int = 0, part: int = 0) -> dict:
    keys = jax.random.split(jax.random.key(seed), 3)
    part_splits = jax.random.split(jax.random.fold_in(keys[2], part), 3)
    return {
        "forward_field": gaussian(part_splits[0], (NX, 2, F, Y * Z), 0.5, 3.0, ((0, 16),)),
        "adjoint_field": gaussian(part_splits[1], (NX, 2, F, Y * Z), 0.5, 3.0, ((0, 16),)),
    }


def correlate(forward_wide, adjoint_wide, cells_kept):
    def per_offset(offset_index):
        source_part = lax.dynamic_slice_in_dim(forward_wide, 2 * HALF - offset_index, cells_kept, 0).astype(jnp.float32)
        receiver_part = lax.dynamic_slice_in_dim(adjoint_wide, offset_index, cells_kept, 0).astype(jnp.float32)
        return jnp.sum(source_part * receiver_part, axis=(1, 2))
    return lax.map(per_offset, jnp.arange(LAGS, dtype=jnp.int32))


def laplace(padded):
    middle = padded[:, 1:-1]
    shaped = middle.reshape(middle.shape[0], middle.shape[1], middle.shape[2] // Z, Z)
    deeper = jnp.pad(shaped, ((0, 0), (0, 0), (0, 0), (1, 1)))
    along_depth = (deeper[..., 2:] + deeper[..., :-2]).reshape(middle.shape)
    return 0.25 * (padded[:, 2:] + padded[:, :-2] + along_depth - 4.0 * middle)


def reference(forward_field, adjoint_field):
    widths = ((HALF, HALF), (0, 0), (0, 0), (0, 0))
    forward_wide = jnp.pad(forward_field, widths)
    adjoint_wide = jnp.pad(adjoint_field, widths)
    offset_image = correlate(forward_wide, adjoint_wide, forward_field.shape[0])
    return laplace(jnp.pad(offset_image, ((0, 0), (1, 1), (0, 0))))
```

```python
import functools

import jax
import jax.numpy as jnp
from jax import lax
from jax.experimental import pallas as pl
from jax.experimental.pallas import tpu as pltpu
from jax.sharding import PartitionSpec as P

Z = 64
HALF = 16
LAGS = 33
BLOCK = 3
OFF = 17
WIDE = 50
LANES = 128
CELLS = 512

CHUNKS = ((16, 1), (5, 4, 3, 2), (11, 10, 9, 8, 7, 6), (14, 13, 12), (15,))
BLOCKS = ((5, 4, 6), (2, 3, 7, 8), (1, 9), (0, 10))


def left_rows(chunk):
    return [-i for i in chunk]


def right_rows(chunk, cells):
    return [cells - 1 + i for i in reversed(chunk)]


def take(field, rows):
    spans, out = [], []
    for r in rows:
        if spans and spans[-1][1] == r:
            spans[-1][1] = r + 1
        else:
            spans.append([r, r + 1])
    for a, b in spans:
        out.append(lax.slice_in_dim(field, a, b, axis=0))
    return out


def correlate_rows(s, r):
    t = s * r
    return jnp.sum(t[:, 0] + t[:, 1], axis=1)


def edge_kernel(a_ref, b_ref, lo_ref, hi_ref):
    def row(ref, k):
        return ref[k : k + 1].astype(jnp.float32)

    lo_ref[0:1] = correlate_rows(row(b_ref, 0), row(a_ref, 2))
    lo_ref[1:2] = correlate_rows(row(a_ref, 0), row(b_ref, 2))
    hi_ref[0:1] = correlate_rows(row(b_ref, 1), row(a_ref, 3))
    hi_ref[1:2] = correlate_rows(row(a_ref, 1), row(b_ref, 3))


def lag_block(blk, nblk, blocks):
    out = jnp.int32(blocks[0])
    for k in range(1, nblk):
        out = jnp.where(blk == k, blocks[k], out)
    return out


def lag_kernel(cells, blocks, places, rim, *refs):
    n_in = len(places)
    ins = refs[:n_in]
    pos = n_in
    if rim:
        lo_ref, hi_ref = refs[pos : pos + 2]
        pos += 2
    if refs[pos].shape[0] == LAGS:
        pos += 1
    out_ref, wide, padded = refs[pos : pos + 3]
    blk = pl.program_id(1)

    @pl.when(blk == 0)
    def _():
        if rim:
            wide[:, 0:1] = jnp.zeros_like(wide[:, 0:1])
            wide[:, WIDE - 1 : WIDE] = jnp.zeros_like(wide[:, 0:1])
        for ref, place in zip(ins, places):
            for src, field, dst, n in place:
                wide[field, dst : dst + n] = ref[src : src + n].astype(jnp.float32)

    base = lag_block(blk, len(blocks), blocks) * BLOCK
    lane = lax.broadcasted_iota(jnp.int32, (cells, LANES), 1) % Z
    first = lane == 0
    last = lane == Z - 1

    def tile(j, _):
        cols = pl.ds(pl.multiple_of(j * LANES, LANES), LANES)

        for t in range(BLOCK):
            h = base + t - HALF
            s = wide[0, pl.ds(OFF - 1 - h, cells + 2), :, :, cols]
            r = wide[1, pl.ds(OFF - 1 + h, cells + 2), :, :, cols]
            u = correlate_rows(s, r)
            padded[7 : 9 + cells] = u
            if rim:
                for at, outer in ((0, h == -HALF), (1, h == HALF)):
                    lo = jnp.where(outer, lo_ref[at : at + 1, cols], 0.0)
                    hi = jnp.where(outer, hi_ref[at : at + 1, cols], 0.0)
                    padded[7:8] = padded[7:8] + lo
                    padded[8 + cells : 9 + cells] = padded[8 + cells : 9 + cells] + hi
            mid = padded[8 : 8 + cells]
            down = jnp.where(first, 0.0, pltpu.roll(mid, 1, 1))
            up = jnp.where(last, 0.0, pltpu.roll(mid, LANES - 1, 1))
            around = padded[7 : 7 + cells] + padded[9 : 9 + cells] + (down + up)
            out_ref[t, :, cols] = 0.25 * (around - 4.0 * mid)
        return 0

    lax.fori_loop(0, CELLS // LANES, tile, 0)


def on_device(forward_field, adjoint_field):
    cells, parts, freqs, width = forward_field.shape
    peers = lax.axis_size("gx")
    up = [(i, (i + 1) % peers) for i in range(peers - 1)]
    down = [(j, i) for i, j in up]
    field_bytes = parts * freqs * width * 2

    from_left, from_right = [], []
    for chunk in CHUNKS:
        to_right = [cells + r for r in left_rows(chunk)]
        to_left = [r - cells for r in right_rows(chunk, cells)]
        sent_up = jnp.concatenate(
            take(forward_field, to_right) + take(adjoint_field, to_right), axis=0
        )
        sent_down = jnp.concatenate(
            take(forward_field, to_left) + take(adjoint_field, to_left), axis=0
        )
        from_left.append(lax.ppermute(sent_up, "gx", up))
        from_right.append(lax.ppermute(sent_down, "gx", down))

    steps = width // CELLS
    rows4 = pl.BlockSpec((4, parts, freqs, CELLS), lambda c: (0, 0, 0, c))
    rim_spec = pl.BlockSpec((2, CELLS), lambda c: (0, c))
    lo, hi = pl.pallas_call(
        edge_kernel,
        grid=(steps,),
        in_specs=[rows4, rows4],
        out_specs=[rim_spec, rim_spec],
        out_shape=[jax.ShapeDtypeStruct((2, width), jnp.float32)] * 2,
        cost_estimate=pl.CostEstimate(
            flops=8 * parts * freqs * width, bytes_accessed=12 * field_bytes, transcendentals=0
        ),
        name="rim",
    )(from_left[0], from_right[0])
    rim_hi = lax.ppermute(lo, "gx", down)
    rim_lo = lax.ppermute(hi, "gx", up)

    image = None
    for stage, blocks in enumerate(BLOCKS):
        reach = max(max(abs(3 * b - HALF), abs(3 * b + 2 - HALF)) for b in blocks)
        rim = reach == HALF
        operands = [forward_field, adjoint_field]
        places = [[(0, 0, OFF, cells)], [(0, 1, OFF, cells)]]
        for g in range(stage + 2):
            n = len(CHUNKS[g])
            for got, rows in (
                (from_left[g], left_rows(CHUNKS[g])),
                (from_right[g], right_rows(CHUNKS[g], cells)),
            ):
                place = []
                for field in (0, 1):
                    k = 0
                    while k < n:
                        m = 1
                        while k + m < n and rows[k + m] == rows[k] + m:
                            m += 1
                        place.append((field * n + k, field, OFF + rows[k], m))
                        k += m
                operands.append(got)
                places.append(place)
        specs = [
            pl.BlockSpec((o.shape[0], parts, freqs, CELLS), lambda c, b: (0, 0, 0, c))
            for o in operands
        ]
        if rim:
            operands += [rim_lo, rim_hi]
            specs += [pl.BlockSpec((2, CELLS), lambda c, b: (0, c))] * 2
        aliases = {}
        if image is not None:
            aliases = {len(operands): 0}
            operands.append(image)
            specs.append(pl.BlockSpec(memory_space=pl.ANY))
        nblk = len(blocks)
        image = pl.pallas_call(
            functools.partial(lag_kernel, cells, blocks, places, rim),
            grid=(steps, nblk),
            in_specs=specs,
            out_specs=pl.BlockSpec(
                (BLOCK, cells, CELLS),
                lambda c, b, nblk=nblk, blocks=blocks: (lag_block(b, nblk, blocks), 0, c),
            ),
            out_shape=jax.ShapeDtypeStruct((LAGS, cells, width), jnp.float32),
            scratch_shapes=[
                pltpu.VMEM((2, WIDE, parts, freqs, CELLS), jnp.float32),
                pltpu.VMEM((32, LANES), jnp.float32),
            ],
            input_output_aliases=aliases,
            compiler_params=pltpu.CompilerParams(vmem_limit_bytes=40 * 2**20),
            cost_estimate=pl.CostEstimate(
                flops=2 * 3 * nblk * (cells + 2) * parts * freqs * width,
                bytes_accessed=3 * nblk * cells * width * 4
                + sum(o.shape[0] for o in operands[: len(places)]) * field_bytes,
                transcendentals=0,
            ),
            name="lags_%d" % stage,
        )(*operands)
    return image


def solution(mesh):
    placed = (P(("shots", "gx"), None, None, None), P(("shots", "gx"), None, None, None))
    return jax.shard_map(
        on_device,
        mesh=mesh,
        in_specs=placed,
        out_specs=P(None, ("shots", "gx"), None),
        check_vma=False,
    )
```

```python
import functools

import jax
import jax.numpy as jnp
from jax import lax
from jax.experimental import pallas as pl
from jax.experimental.pallas import tpu as pltpu
from jax.sharding import PartitionSpec as P

Z = 64
HALF = 16
LAGS = 33
BLOCK = 3
LANES = 128
SUB = 16
SPAN = 6
RATE = 200

CHUNKS = ((16, 1), (5, 4, 3, 2), (11, 10, 9, 8, 7, 6), (14, 13, 12), (15,))
BLOCKS = ((5, 4, 6), (2, 3, 7, 8), (1, 9), (0, 10))

VMEM = pl.BlockSpec(memory_space=pltpu.VMEM)
ANY = pl.BlockSpec(memory_space=pl.ANY)


def left_rows(chunk):
    return [-i for i in chunk]


def right_rows(chunk, cells):
    return [cells - 1 + i for i in reversed(chunk)]


def take(field, rows):
    spans = []
    for r in rows:
        if spans and spans[-1][1] == r:
            spans[-1][1] = r + 1
        else:
            spans.append([r, r + 1])
    return [lax.slice_in_dim(field, a, b, axis=0) for a, b in spans]


def pack_kernel(s_ref, r_ref, so_ref, ro_ref, flip):
    rows, parts, freqs, width = s_ref.shape
    for row in range(rows):
        for field, (src, dst) in enumerate(((s_ref, so_ref), (r_ref, ro_ref))):
            for p in range(parts):
                for g in range(width // (SUB * LANES)):
                    slot = flip.at[(field * parts + p) * 2 + g % 2]
                    for t in range(SUB):
                        c = (g * SUB + t) * LANES
                        slot[pl.ds(t, freqs, SUB), :] = src[row, p, :, c : c + LANES].astype(
                            jnp.float32
                        )
                    for f in range(freqs):
                        dst[row, p * freqs + f, g * SUB : (g + 1) * SUB] = slot[
                            f * SUB : (f + 1) * SUB
                        ].astype(jnp.bfloat16)


def pack(forward_field, adjoint_field):
    cells, parts, freqs, width = forward_field.shape
    rows = 2
    spec = pl.BlockSpec((rows, parts, freqs, width), lambda i: (i, 0, 0, 0))
    tiles = width // LANES
    out = pl.BlockSpec((rows, parts * freqs, tiles, LANES), lambda i: (i, 0, 0, 0))
    shape = jax.ShapeDtypeStruct((cells, parts * freqs, tiles, LANES), jnp.bfloat16)
    return pl.pallas_call(
        pack_kernel,
        grid=(cells // rows,),
        in_specs=[spec, spec],
        out_specs=[out, out],
        out_shape=[shape, shape],
        scratch_shapes=[pltpu.VMEM((4 * parts, SUB * freqs, LANES), jnp.float32)],
        cost_estimate=pl.CostEstimate(
            flops=0, bytes_accessed=8 * cells * parts * freqs * width, transcendentals=0
        ),
        name="pack",
    )(forward_field, adjoint_field)


def rim_kernel(a_ref, b_ref, lo_ref, hi_ref):
    def dot(s, r):
        total = s[0].astype(jnp.float32) * r[0].astype(jnp.float32)
        for k in range(1, s.shape[0]):
            total += s[k].astype(jnp.float32) * r[k].astype(jnp.float32)
        return total

    def tile(g, _):
        at = pl.ds(pl.multiple_of(g * SUB, SUB), SUB)
        lo_ref[0, at] = dot(b_ref.at[0, :, at], a_ref.at[2, :, at])
        lo_ref[1, at] = dot(a_ref.at[0, :, at], b_ref.at[2, :, at])
        hi_ref[0, at] = dot(b_ref.at[1, :, at], a_ref.at[3, :, at])
        hi_ref[1, at] = dot(a_ref.at[1, :, at], b_ref.at[3, :, at])
        return 0

    lax.fori_loop(0, a_ref.shape[2] // SUB, tile, 0)


def lag_kernel(cells, blocks, where, rim, aliased, *refs):
    refs = list(refs)
    ins = [refs.pop(0) for _ in range(1 + max(w[0] for w in where.values()))]
    rims = [refs.pop(0) for _ in range(2)] if rim else None
    if aliased:
        refs.pop(0)
    out_ref, sums, flip, ready, sems = refs
    terms, tiles = ins[0].shape[1], ins[0].shape[2]
    lane = lax.broadcasted_iota(jnp.int32, (SUB, LANES), 1) % Z
    first = lane == 0
    last = lane == Z - 1

    def copies(n, g):
        cols = pl.ds(pl.multiple_of(g * (SUB * LANES), SUB * LANES), SUB * LANES)
        return pltpu.make_async_copy(
            ready.at[n, g],
            out_ref.at[pl.ds(blocks[n] * BLOCK, BLOCK), :, cols],
            sems.at[n, g],
        )

    def tile(g, _):
        at = pl.ds(pl.multiple_of(g * SUB, SUB), SUB)

        for n, blk in enumerate(blocks):
            lags = [blk * BLOCK + t - HALF for t in range(BLOCK)]
            for x0 in range(-1, cells + 1, SPAN):
                pairs = [
                    (t, x)
                    for t in range(BLOCK)
                    for x in range(x0, x0 + SPAN)
                    if (0, x - lags[t]) in where and (1, x + lags[t]) in where
                ]
                pairs.sort(key=lambda p: (p[1] - lags[p[0]], p[1]))

                def step(k, accs):
                    got = {}

                    def row(field, a):
                        if (field, a) not in got:
                            n_in, src = where[field, a]
                            got[field, a] = ins[n_in][src, k, at].astype(jnp.float32)
                        return got[field, a]

                    return tuple(
                        acc + row(0, x - lags[t]) * row(1, x + lags[t])
                        for acc, (t, x) in zip(accs, pairs)
                    )

                zero = jnp.zeros((SUB, LANES), jnp.float32)
                accs = lax.fori_loop(0, terms, step, (zero,) * len(pairs))
                for acc, (t, x) in zip(accs, pairs):
                    sums[t, x + 1] = acc
            for t in range(BLOCK):
                if abs(lags[t]) == HALF:
                    sums[t, 0] = rims[0][int(lags[t] > 0), at]
                    sums[t, cells + 1] = rims[1][int(lags[t] > 0), at]
                for x in range(cells):
                    mid = sums[t, x + 1]
                    down = jnp.where(first, 0.0, pltpu.roll(mid, 1, 1))
                    up = jnp.where(last, 0.0, pltpu.roll(mid, LANES - 1, 1))
                    around = (sums[t, x] + sums[t, x + 2]) + (down + up)
                    flip[t, pl.ds(x, SUB, cells), :] = 0.25 * (around - 4.0 * mid)
                for c in range(SUB):
                    ready[n, g, t, :, c * LANES : (c + 1) * LANES] = flip[
                        t, c * cells : (c + 1) * cells
                    ]
            copies(n, g).start()
        return 0

    groups = tiles // SUB
    lax.fori_loop(0, groups, tile, 0)
    for n in range(len(blocks)):
        for g in range(groups):
            copies(n, g).wait()


def on_device(forward_field, adjoint_field):
    cells, parts, freqs, width = forward_field.shape
    terms, tiles = parts * freqs, width // LANES
    peers = lax.axis_size("gx")
    up = [(i, (i + 1) % peers) for i in range(peers - 1)]
    down = [(j, i) for i, j in up]
    field_bytes = terms * width * 2

    source, receiver = pack(forward_field, adjoint_field)

    from_left, from_right = [], []
    for g, chunk in enumerate(CHUNKS):
        to_right = [cells + r for r in left_rows(chunk)]
        to_left = [r - cells for r in right_rows(chunk, cells)]
        sent_up = jnp.concatenate(take(source, to_right) + take(receiver, to_right), axis=0)
        sent_down = jnp.concatenate(take(source, to_left) + take(receiver, to_left), axis=0)
        if g >= 2:
            sent_up, sent_down, from_left[g - 2], from_right[g - 2] = lax.optimization_barrier(
                (sent_up, sent_down, from_left[g - 2], from_right[g - 2])
            )
        from_left.append(lax.ppermute(sent_up, "gx", up))
        from_right.append(lax.ppermute(sent_down, "gx", down))

    lo, hi = pl.pallas_call(
        rim_kernel,
        in_specs=[VMEM, VMEM],
        out_specs=[VMEM, VMEM],
        out_shape=[jax.ShapeDtypeStruct((2, tiles, LANES), jnp.float32)] * 2,
        cost_estimate=pl.CostEstimate(
            flops=8 * terms * width, bytes_accessed=12 * field_bytes, transcendentals=0
        ),
        name="rim",
    )(from_left[0], from_right[0])
    rim_hi = lax.ppermute(lo, "gx", down)
    rim_lo = lax.ppermute(hi, "gx", up)

    image = None
    for stage, blocks in enumerate(BLOCKS):
        rim = 0 in blocks
        operands = [source, receiver]
        where = {(field, a): (field, a) for field in (0, 1) for a in range(cells)}
        for g in range(stage + 2):
            n = len(CHUNKS[g])
            for got, rows in (
                (from_left[g], left_rows(CHUNKS[g])),
                (from_right[g], right_rows(CHUNKS[g], cells)),
            ):
                for field in (0, 1):
                    for k, a in enumerate(rows):
                        where[field, a] = (len(operands), field * n + k)
                operands.append(got)
        n_fields = len(operands)
        if rim:
            operands += [rim_lo, rim_hi]
        specs = [VMEM] * len(operands)
        aliases = {}
        if image is not None:
            aliases = {len(operands): 0}
            operands.append(image)
            specs.append(ANY)
        nblk = len(blocks)
        groups = tiles // SUB
        image = pl.pallas_call(
            functools.partial(lag_kernel, cells, blocks, where, rim, image is not None),
            in_specs=specs,
            out_specs=ANY,
            out_shape=jax.ShapeDtypeStruct((LAGS, cells, width), jnp.float32),
            scratch_shapes=[
                pltpu.VMEM((BLOCK, cells + 2, SUB, LANES), jnp.float32),
                pltpu.VMEM((BLOCK, SUB * cells, LANES), jnp.float32),
                pltpu.VMEM((nblk, groups, BLOCK, cells, SUB * LANES), jnp.float32),
                pltpu.SemaphoreType.DMA((nblk, groups)),
            ],
            input_output_aliases=aliases,
            compiler_params=pltpu.CompilerParams(vmem_limit_bytes=36 * 2**20),
            cost_estimate=pl.CostEstimate(
                flops=RATE * 2 * 3 * nblk * (cells + 2) * terms * width,
                bytes_accessed=3 * nblk * cells * width * 4
                + sum(o.shape[0] for o in operands[:n_fields]) * field_bytes,
                transcendentals=0,
            ),
            name="lags_%d" % stage,
        )(*operands)
    return image


def solution(mesh):
    placed = (P(("shots", "gx"), None, None, None), P(("shots", "gx"), None, None, None))
    return jax.shard_map(
        on_device,
        mesh=mesh,
        in_specs=placed,
        out_specs=P(None, ("shots", "gx"), None),
        check_vma=False,
    )
```

```python
import functools

import jax
import jax.numpy as jnp
from jax import lax
from jax.experimental import pallas as pl
from jax.experimental.pallas import tpu as pltpu
from jax.sharding import PartitionSpec as P

Z = 64
HALF = 16
LAGS = 33
BLOCK = 3
LANES = 128
SUB = 16
SPAN = 3
RATE = 200

CHUNKS = ((16, 2, 1), (5, 4, 3), (8, 7, 6), (14, 13, 12, 11, 10, 9), (15,))
BUNDLES = ((0, 1), (2,))
BLOCKS = ((1, (5, 4, 6)), (2, (3, 7)), (3, (2, 8, 1, 9)), (4, (0, 10)))

VMEM = pl.BlockSpec(memory_space=pltpu.VMEM)
ANY = pl.BlockSpec(memory_space=pl.ANY)


def left_rows(chunk):
    return [-i for i in chunk]


def right_rows(chunk, cells):
    return [cells - 1 + i for i in reversed(chunk)]


def take(field, rows):
    spans = []
    for r in rows:
        if spans and spans[-1][1] == r:
            spans[-1][1] = r + 1
        else:
            spans.append([r, r + 1])
    return [lax.slice_in_dim(field, a, b, axis=0) for a, b in spans]


def pack_kernel(s_ref, r_ref, so_ref, ro_ref, flip):
    rows, parts, freqs, width = s_ref.shape
    for row in range(rows):
        for field, (src, dst) in enumerate(((s_ref, so_ref), (r_ref, ro_ref))):
            for p in range(parts):
                for g in range(width // (SUB * LANES)):
                    slot = flip.at[(field * parts + p) * 2 + g % 2]
                    for t in range(SUB):
                        c = (g * SUB + t) * LANES
                        slot[pl.ds(t, freqs, SUB), :] = src[row, p, :, c : c + LANES].astype(
                            jnp.float32
                        )
                    for f in range(freqs):
                        dst[row, p * freqs + f, g * SUB : (g + 1) * SUB] = slot[
                            f * SUB : (f + 1) * SUB
                        ].astype(jnp.bfloat16)


def pack(forward_field, adjoint_field):
    cells, parts, freqs, width = forward_field.shape
    rows = 2
    spec = pl.BlockSpec((rows, parts, freqs, width), lambda i: (i, 0, 0, 0))
    tiles = width // LANES
    out = pl.BlockSpec((rows, parts * freqs, tiles, LANES), lambda i: (i, 0, 0, 0))
    shape = jax.ShapeDtypeStruct((cells, parts * freqs, tiles, LANES), jnp.bfloat16)
    return pl.pallas_call(
        pack_kernel,
        grid=(cells // rows,),
        in_specs=[spec, spec],
        out_specs=[out, out],
        out_shape=[shape, shape],
        scratch_shapes=[pltpu.VMEM((4 * parts, SUB * freqs, LANES), jnp.float32)],
        cost_estimate=pl.CostEstimate(
            flops=0, bytes_accessed=8 * cells * parts * freqs * width, transcendentals=0
        ),
        name="pack",
    )(forward_field, adjoint_field)


def rim_kernel(cells, where, *refs):
    ins, (lo_ref, hi_ref) = refs[:-2], refs[-2:]

    def tile(g, _):
        at = pl.ds(pl.multiple_of(g * SUB, SUB), SUB)

        def dot(a, b):
            (s_in, s), (r_in, r) = where[0, a], where[1, b]
            total = jnp.zeros((SUB, LANES), jnp.float32)
            for k in range(ins[0].shape[1]):
                total += ins[s_in][s, k, at].astype(jnp.float32) * ins[r_in][r, k, at].astype(
                    jnp.float32
                )
            return total

        for ref, x in ((lo_ref, 0), (hi_ref, cells - 1)):
            ref[0, at] = dot(x + HALF, x - HALF)
            ref[1, at] = dot(x - HALF, x + HALF)
        return 0

    lax.fori_loop(0, ins[0].shape[2] // SUB, tile, 0)


def lag_kernel(cells, blocks, where, rim, aliased, *refs):
    refs = list(refs)
    ins = [refs.pop(0) for _ in range(1 + max(w[0] for w in where.values()))]
    rims = [refs.pop(0) for _ in range(2)] if rim else None
    if aliased:
        refs.pop(0)
    out_ref, sums, flip, ready, sems = refs
    terms, tiles = ins[0].shape[1], ins[0].shape[2]
    lane = lax.broadcasted_iota(jnp.int32, (SUB, LANES), 1) % Z
    first = lane == 0
    last = lane == Z - 1

    def copies(n, g):
        cols = pl.ds(pl.multiple_of(g * (SUB * LANES), SUB * LANES), SUB * LANES)
        return pltpu.make_async_copy(
            ready.at[n, g],
            out_ref.at[pl.ds(blocks[n] * BLOCK, BLOCK), :, cols],
            sems.at[n, g],
        )

    def tile(g, _):
        at = pl.ds(pl.multiple_of(g * SUB, SUB), SUB)

        for n, blk in enumerate(blocks):
            lags = [blk * BLOCK + t - HALF for t in range(BLOCK)]
            for x0 in range(-1, cells + 1, SPAN):
                pairs = [
                    (t, x)
                    for t in range(BLOCK)
                    for x in range(x0, x0 + SPAN)
                    if (0, x - lags[t]) in where and (1, x + lags[t]) in where
                ]
                pairs.sort(key=lambda p: (p[1] - lags[p[0]], p[1]))

                def step(k, accs):
                    got = {}

                    def row(field, a):
                        if (field, a) not in got:
                            n_in, src = where[field, a]
                            got[field, a] = ins[n_in][src, k, at].astype(jnp.float32)
                        return got[field, a]

                    return tuple(
                        acc + row(0, x - lags[t]) * row(1, x + lags[t])
                        for acc, (t, x) in zip(accs, pairs)
                    )

                zero = jnp.zeros((SUB, LANES), jnp.float32)
                accs = lax.fori_loop(0, terms, step, (zero,) * len(pairs), unroll=terms)
                for acc, (t, x) in zip(accs, pairs):
                    sums[t, x + 1] = acc
            for t in range(BLOCK):
                if abs(lags[t]) == HALF:
                    sums[t, 0] = rims[0][int(lags[t] > 0), at]
                    sums[t, cells + 1] = rims[1][int(lags[t] > 0), at]
                for x in range(cells):
                    mid = sums[t, x + 1]
                    down = jnp.where(first, 0.0, pltpu.roll(mid, 1, 1))
                    up = jnp.where(last, 0.0, pltpu.roll(mid, LANES - 1, 1))
                    around = (sums[t, x] + sums[t, x + 2]) + (down + up)
                    flip[t, pl.ds(x, SUB, cells), :] = 0.25 * (around - 4.0 * mid)
                for c in range(SUB):
                    ready[n, g, t, :, c * LANES : (c + 1) * LANES] = flip[
                        t, c * cells : (c + 1) * cells
                    ]
            copies(n, g).start()
        return 0

    groups = tiles // SUB
    lax.fori_loop(0, groups, tile, 0)
    for n in range(len(blocks)):
        for g in range(groups):
            copies(n, g).wait()


def neighbours(peers):
    up = [(i, i + 1) for i in range(peers - 1)]
    return up, [(j, i) for i, j in up]


def routes(peers, chunk):
    up, down = neighbours(peers)
    if peers != 16 or chunk > 2:
        return up, down, (), ()
    steps = peers // 4
    far_up = range(0, steps - 1 - chunk)
    far_down = range(chunk, steps - 1)
    up = [p for p in up if p not in [(4 * z + 3, 4 * z + 4) for z in far_up]]
    up += [(4 * z + 3, 4 * z) for z in far_up]
    down = [p for p in down if p not in [(4 * z + 4, 4 * z + 3) for z in far_down]]
    down += [(4 * z + 4, 4 * z + 7) for z in far_down]
    swap_up = sorted({4 * z for z in far_up} | {4 * z + 4 for z in far_up})
    swap_down = sorted({4 * z + 7 for z in far_down} | {4 * z + 3 for z in far_down})
    return up, down, swap_up, swap_down


def is_one_of(me, devices):
    found = jnp.bool_(False)
    for d in devices:
        found |= me == d
    return found


def on_device(forward_field, adjoint_field):
    cells, parts, freqs, width = forward_field.shape
    terms, tiles = parts * freqs, width // LANES
    peers = lax.axis_size("gx")
    me = lax.axis_index("gx")
    plain_up, plain_down = neighbours(peers)
    field_bytes = terms * width * 2

    def outgoing(source, receiver, chunk):
        to_right = [cells + r for r in left_rows(chunk)]
        to_left = [r - cells for r in right_rows(chunk, cells)]
        return (
            jnp.concatenate(take(source, to_right) + take(receiver, to_right), axis=0),
            jnp.concatenate(take(source, to_left) + take(receiver, to_left), axis=0),
        )

    def send(pair, g):
        up, down, _, _ = routes(peers, g)
        return lax.ppermute(pair[0], "gx", up), lax.ppermute(pair[1], "gx", down)

    def after(values, earlier):
        out = lax.optimization_barrier((*values, *earlier))
        return out[:2], out[2:]

    arrived = [send(outgoing(forward_field, adjoint_field, CHUNKS[0]), 0)]
    source, receiver = pack(forward_field, adjoint_field)
    for g in range(1, len(CHUNKS)):
        sent = outgoing(source, receiver, CHUNKS[g])
        if g >= 2:
            sent, arrived[g - 2] = after(sent, arrived[g - 2])
        arrived.append(send(sent, g))
    arrived[0] = pack(*arrived[0])

    pieces = []
    for bundle in BUNDLES:
        got = [jnp.concatenate([arrived[g][side] for g in bundle], axis=0) for side in (0, 1)]
        if peers == 16:
            hop_up = [(4 * z, 4 * z + 4) for z in range(peers // 4 - 1)]
            hop_down = [(4 * z + 7, 4 * z + 3) for z in range(peers // 4 - 1)]
            hops = [lax.ppermute(got[0], "gx", hop_up), lax.ppermute(got[1], "gx", hop_down)]
            for side in (0, 1):
                swapped = jnp.concatenate(
                    [
                        jnp.broadcast_to(
                            is_one_of(me, routes(peers, g)[2 + side]), (2 * len(CHUNKS[g]),)
                        )
                        for g in bundle
                    ]
                )
                got[side] = jnp.where(swapped[:, None, None, None], hops[side], got[side])
        pieces.append((bundle, got))
    for g in range(3, len(CHUNKS)):
        pieces.append(((g,), list(arrived[g])))

    def layout(count, own):
        operands = [source, receiver] if own else []
        where = {(f, a): (f, a) for f in (0, 1) for a in range(cells)} if own else {}
        for bundle, got in pieces[:count]:
            for side in (0, 1):
                base = 0
                for g in bundle:
                    n = len(CHUNKS[g])
                    rows = right_rows(CHUNKS[g], cells) if side else left_rows(CHUNKS[g])
                    for field in (0, 1):
                        for k, a in enumerate(rows):
                            where[field, a] = (len(operands), base + field * n + k)
                    base += 2 * n
                operands.append(got[side])
        return operands, where

    operands, where = layout(1, False)
    lo, hi = pl.pallas_call(
        functools.partial(rim_kernel, cells, where),
        in_specs=[VMEM] * len(operands),
        out_specs=[VMEM, VMEM],
        out_shape=[jax.ShapeDtypeStruct((2, tiles, LANES), jnp.float32)] * 2,
        cost_estimate=pl.CostEstimate(
            flops=RATE * 8 * terms * width, bytes_accessed=12 * field_bytes, transcendentals=0
        ),
        name="rim",
    )(*operands)
    rim_hi = lax.ppermute(lo, "gx", plain_down)
    rim_lo = lax.ppermute(hi, "gx", plain_up)

    image = None
    for stage, (count, blocks) in enumerate(BLOCKS):
        rim = 0 in blocks
        operands, where = layout(count, True)
        n_fields = len(operands)
        if rim:
            operands += [rim_lo, rim_hi]
        specs = [VMEM] * len(operands)
        aliases = {}
        if image is not None:
            aliases = {len(operands): 0}
            operands.append(image)
            specs.append(ANY)
        nblk = len(blocks)
        groups = tiles // SUB
        image = pl.pallas_call(
            functools.partial(lag_kernel, cells, blocks, where, rim, image is not None),
            in_specs=specs,
            out_specs=ANY,
            out_shape=jax.ShapeDtypeStruct((LAGS, cells, width), jnp.float32),
            scratch_shapes=[
                pltpu.VMEM((BLOCK, cells + 2, SUB, LANES), jnp.float32),
                pltpu.VMEM((BLOCK, SUB * cells, LANES), jnp.float32),
                pltpu.VMEM((nblk, groups, BLOCK, cells, SUB * LANES), jnp.float32),
                pltpu.SemaphoreType.DMA((nblk, groups)),
            ],
            input_output_aliases=aliases,
            compiler_params=pltpu.CompilerParams(vmem_limit_bytes=36 * 2**20),
            cost_estimate=pl.CostEstimate(
                flops=RATE * 2 * 3 * nblk * (cells + 2) * terms * width,
                bytes_accessed=3 * nblk * cells * width * 4
                + sum(o.shape[0] for o in operands[:n_fields]) * field_bytes,
                transcendentals=0,
            ),
            name="lags_%d" % stage,
        )(*operands)
    return image


def solution(mesh):
    placed = (P(("shots", "gx"), None, None, None), P(("shots", "gx"), None, None, None))
    return jax.shard_map(
        on_device,
        mesh=mesh,
        in_specs=placed,
        out_specs=P(None, ("shots", "gx"), None),
        check_vma=False,
    )
```

```python
import functools

import jax
import jax.numpy as jnp
from jax import lax
from jax.experimental import pallas as pl
from jax.experimental.pallas import tpu as pltpu
from jax.sharding import PartitionSpec as P

Z = 64
HALF = 16
LAGS = 33
BLOCK = 3
LANES = 128
SUB = 16
SPAN = 3
RATE = 50

CHUNKS = ((16, 2, 1), (5, 4, 3), (8, 7, 6), (15, 14, 13, 12, 11, 10, 9))
BUNDLES = ((0, 1), (2,))
NEAR = ((1, (5, 4, 6)), (2, (3, 7)))
FAR = (2, 8, 1, 9, 0, 10)

VMEM = pl.BlockSpec(memory_space=pltpu.VMEM)
ANY = pl.BlockSpec(memory_space=pl.ANY)


SMEM = pl.BlockSpec(memory_space=pltpu.SMEM)


def pack_kernel(core_ref, s_ref, r_ref, out_ref, flip):
    _, parts, freqs, width = s_ref.shape
    for field, src in enumerate((s_ref, r_ref)):
        for p in range(parts):
            for g in range(width // (SUB * LANES)):
                slot = flip.at[(field * parts + p) * 2 + g % 2]
                for t in range(SUB):
                    c = (g * SUB + t) * LANES
                    slot[pl.ds(t, freqs, SUB), :] = src[0, p, :, c : c + LANES].astype(jnp.float32)
                for f in range(freqs):
                    out_ref[0, field, p * freqs + f, g * SUB : (g + 1) * SUB] = slot[
                        f * SUB : (f + 1) * SUB
                    ].astype(jnp.bfloat16)


def pack(core, forward_field, adjoint_field):
    cells, parts, freqs, width = forward_field.shape
    spec = pl.BlockSpec(
        (1, parts, freqs, width),
        lambda i, core: (jnp.where(core[0] == 1, i, cells - 1 - i), 0, 0, 0),
    )
    tiles = width // LANES
    return pl.pallas_call(
        pack_kernel,
        grid_spec=pltpu.PrefetchScalarGridSpec(
            num_scalar_prefetch=1,
            grid=(cells,),
            in_specs=[spec, spec],
            out_specs=pl.BlockSpec(
                (1, 2, parts * freqs, tiles, LANES), lambda i, core: (i, 0, 0, 0, 0)
            ),
            scratch_shapes=[pltpu.VMEM((4 * parts, SUB * freqs, LANES), jnp.float32)],
        ),
        out_shape=jax.ShapeDtypeStruct((cells, 2, parts * freqs, tiles, LANES), jnp.bfloat16),
        cost_estimate=pl.CostEstimate(
            flops=0, bytes_accessed=8 * cells * parts * freqs * width, transcendentals=0
        ),
        name="pack",
    )(core, forward_field, adjoint_field)


def rim_kernel(cells, where, *refs):
    ins, (lo_ref, hi_ref) = refs[:-2], refs[-2:]

    def tile(g, _):
        at = pl.ds(pl.multiple_of(g * SUB, SUB), SUB)

        def dot(a, b):
            (s_in, s), (r_in, r) = where[a], where[b]
            total = jnp.zeros((SUB, LANES), jnp.float32)
            for k in range(ins[0].shape[2]):
                total += ins[s_in][s, 0, k, at].astype(jnp.float32) * ins[r_in][
                    r, 1, k, at
                ].astype(jnp.float32)
            return total

        for ref, x in ((lo_ref, 0), (hi_ref, cells - 1)):
            ref[0, at] = dot(x - HALF, x + HALF)
            ref[1, at] = dot(x + HALF, x - HALF)
        return 0

    lax.fori_loop(0, ins[0].shape[3] // SUB, tile, 0)


def sum_pairs(ins, where, lags, pairs, k_count, at, init):
    pairs = sorted(pairs, key=lambda p: (p[1] // SPAN, p[1] - lags[p[0]], p[1]))

    def step(k, accs):
        got = {}

        def row(field, a):
            if (field, a) not in got:
                n_in, src = where[a]
                got[field, a] = ins[n_in][src, field, k, at].astype(jnp.float32)
            return got[field, a]

        return tuple(
            acc + row(0, x - lags[t]) * row(1, x + lags[t]) for acc, (t, x) in zip(accs, pairs)
        )

    accs = lax.fori_loop(0, k_count, step, tuple(init(*p) for p in pairs), unroll=k_count)
    return zip(pairs, accs)


def blocks_of(cells, lags, keep):
    spans = []
    for x0 in range(-1, cells + 1, SPAN):
        pairs = [
            (t, x)
            for t in range(BLOCK)
            for x in range(x0, x0 + SPAN)
            if (abs(lags[t]) < HALF or 0 <= x < cells) and keep(x - lags[t], x + lags[t])
        ]
        if spans and len(spans[-1]) + len(pairs) <= BLOCK * SPAN:
            spans[-1] += pairs
        elif pairs:
            spans.append(pairs)
    return spans


def part_kernel(cells, blocks, where, *refs):
    ins, out_ref = refs[:-1], refs[-1]
    terms, tiles = ins[0].shape[2], ins[0].shape[3]
    zero = jnp.zeros((SUB, LANES), jnp.float32)

    def tile(g, _):
        at = pl.ds(pl.multiple_of(g * SUB, SUB), SUB)
        for n, blk in enumerate(blocks):
            lags = [blk * BLOCK + t - HALF for t in range(BLOCK)]
            for pairs in blocks_of(cells, lags, lambda a, b: a in where and b in where):
                for (t, x), acc in sum_pairs(
                    ins, where, lags, pairs, terms, at, lambda t, x: zero
                ):
                    out_ref[n, t, x + 1, at] = acc
        return 0

    lax.fori_loop(0, tiles // SUB, tile, 0)


def lag_kernel(cells, blocks, where, early, aliased, *refs):
    refs = list(refs)
    core = refs.pop(0)[0]
    ins = [refs.pop(0) for _ in range(1 + max(w[0] for w in where.values()))]
    if early is not None:
        partial = refs.pop(0)
        rims = [refs.pop(0) for _ in range(2)]
    if aliased:
        refs.pop(0)
    out_ref, sums, flip, ready, sems = refs
    terms, tiles = ins[0].shape[2], ins[0].shape[3]
    lane = lax.broadcasted_iota(jnp.int32, (SUB, LANES), 1) % Z
    first = lane == 0
    last = lane == Z - 1
    zero = jnp.zeros((SUB, LANES), jnp.float32)
    straight = core == 1

    def copies(n, g):
        cols = pl.ds(pl.multiple_of(g * (SUB * LANES), SUB * LANES), SUB * LANES)
        low = jnp.where(straight, blocks[n] * BLOCK, LAGS - (blocks[n] + 1) * BLOCK)
        return pltpu.make_async_copy(
            ready.at[n, g], out_ref.at[pl.ds(low, BLOCK), :, cols], sems.at[n, g]
        )

    def keep(a, b):
        return early is None or a not in early or b not in early

    def tile(g, _):
        at = pl.ds(pl.multiple_of(g * SUB, SUB), SUB)
        for n, blk in enumerate(blocks):
            lags = [blk * BLOCK + t - HALF for t in range(BLOCK)]
            new = set()

            def init(t, x):
                return zero

            for pairs in blocks_of(cells, lags, keep):
                new |= set(pairs)
                for (t, x), acc in sum_pairs(ins, where, lags, pairs, terms, at, init):
                    sums[t, x + 1] = acc

            def value(t, x):
                if abs(lags[t]) == HALF and not 0 <= x < cells:
                    return rims[int(x > 0)][int(lags[t] > 0), at]
                if (t, x) in new:
                    return sums[t, x + 1]
                return partial[n, t, x + 1, at]

            for t in range(BLOCK):
                for x in range(cells):
                    mid = value(t, x)
                    down = jnp.where(first, 0.0, pltpu.roll(mid, 1, 1))
                    up = jnp.where(last, 0.0, pltpu.roll(mid, LANES - 1, 1))
                    around = (value(t, x - 1) + value(t, x + 1)) + (down + up)
                    to = jnp.where(straight, x, cells - 1 - x)
                    flip[t, pl.ds(to, SUB, cells), :] = 0.25 * (around - 4.0 * mid)
                lag = jnp.where(straight, t, BLOCK - 1 - t)
                for c in range(SUB):
                    ready[n, g, lag, :, c * LANES : (c + 1) * LANES] = flip[
                        t, c * cells : (c + 1) * cells
                    ]
            copies(n, g).start()
        return 0

    groups = tiles // SUB
    lax.fori_loop(0, groups, tile, 0)
    for n in range(len(blocks)):
        for g in range(groups):
            copies(n, g).wait()


def exchange(peers):
    up = [(i, i + 1) for i in range(1, peers - 1, 2)]
    return up, [(j, i) for i, j in up]


def routes(peers, chunk):
    up, down = exchange(peers)
    if peers != 16 or chunk > 2:
        return up + down, ()
    steps = peers // 4
    far_up = range(0, steps - 1 - chunk)
    far_down = range(chunk, steps - 1)
    up = [p for p in up if p not in [(4 * z + 3, 4 * z + 4) for z in far_up]]
    up += [(4 * z + 3, 4 * z) for z in far_up]
    down = [p for p in down if p not in [(4 * z + 4, 4 * z + 3) for z in far_down]]
    down += [(4 * z + 4, 4 * z + 7) for z in far_down]
    swap = {4 * z for z in far_up} | {4 * z + 4 for z in far_up}
    swap |= {4 * z + 7 for z in far_down} | {4 * z + 3 for z in far_down}
    return up + down, sorted(swap)


def is_one_of(me, devices):
    found = jnp.bool_(False)
    for d in devices:
        found |= me == d
    return found


def on_device(forward_field, adjoint_field):
    cells, parts, freqs, width = forward_field.shape
    terms, tiles = parts * freqs, width // LANES
    peers = lax.axis_size("gx")
    me = lax.axis_index("gx")
    core = (me % 2).astype(jnp.int32).reshape(1)
    cores = [(i, i + 1) for i in range(0, peers, 2)] + [(i + 1, i) for i in range(0, peers, 2)]
    links = sum(exchange(peers), [])
    row_bytes = 2 * terms * width * 2

    own = pack(core, forward_field, adjoint_field)
    arrived = []
    for g, chunk in enumerate(CHUNKS):
        spans = []
        for i in chunk:
            r = cells - i
            if spans and spans[-1][1] == r:
                spans[-1][1] = r + 1
            else:
                spans.append([r, r + 1])
        sent = jnp.concatenate([lax.slice_in_dim(own, a, b, axis=0) for a, b in spans], axis=0)
        arrived.append(lax.ppermute(sent, "gx", routes(peers, g)[0]))
    beside = lax.ppermute(own, "gx", cores)

    pieces = []
    for bundle in BUNDLES:
        got = jnp.concatenate([arrived[g] for g in bundle], axis=0) if len(bundle) > 1 else arrived[bundle[0]]
        if peers == 16:
            steps = peers // 4
            hop = [(4 * z, 4 * z + 4) for z in range(steps - 1)]
            hop += [(4 * z + 7, 4 * z + 3) for z in range(steps - 1)]
            relayed = lax.ppermute(got, "gx", hop)
            swapped = jnp.concatenate(
                [
                    jnp.broadcast_to(is_one_of(me, routes(peers, g)[1]), (len(CHUNKS[g]),))
                    for g in bundle
                ]
            )
            got = jnp.where(swapped[:, None, None, None, None], relayed, got)
        pieces.append((bundle, got))
    for g in range(1 + BUNDLES[-1][-1], len(CHUNKS)):
        pieces.append(((g,), arrived[g]))

    def layout(count):
        operands = [own, beside]
        where = {a: (0, a) for a in range(cells)}
        where.update({-1 - a: (1, a) for a in range(cells)})
        for bundle, got in pieces[:count]:
            order = [i for g in bundle for i in CHUNKS[g]]
            where.update({cells - 1 + i: (len(operands), k) for k, i in enumerate(order)})
            operands.append(got)
        return operands, where

    operands, where = layout(1)
    lo, hi = pl.pallas_call(
        functools.partial(rim_kernel, cells, where),
        in_specs=[VMEM] * len(operands),
        out_specs=[VMEM, VMEM],
        out_shape=[jax.ShapeDtypeStruct((2, tiles, LANES), jnp.float32)] * 2,
        cost_estimate=pl.CostEstimate(
            flops=RATE * 8 * terms * width, bytes_accessed=6 * row_bytes, transcendentals=0
        ),
        name="rim",
    )(*operands)
    rim_lo = lax.ppermute(lo, "gx", cores)
    rim_hi = lax.ppermute(hi, "gx", links)

    def cost(operands, nblk, share):
        return pl.CostEstimate(
            flops=int(share * RATE * 2 * 3 * nblk * (cells + 2) * terms * width),
            bytes_accessed=3 * nblk * cells * width * 4
            + sum(o.shape[0] for o in operands) * row_bytes,
            transcendentals=0,
        )

    groups = tiles // SUB

    def lags(name, image, blocks, operands, where, early, extra):
        specs = [SMEM] + [VMEM] * (len(operands) + len(extra))
        operands = [core] + operands + extra
        aliases = {}
        if image is not None:
            aliases = {len(operands): 0}
            operands.append(image)
            specs.append(ANY)
        nblk = len(blocks)
        return pl.pallas_call(
            functools.partial(lag_kernel, cells, blocks, where, early, image is not None),
            in_specs=specs,
            out_specs=ANY,
            out_shape=jax.ShapeDtypeStruct((LAGS, cells, width), jnp.float32),
            scratch_shapes=[
                pltpu.VMEM((BLOCK, cells + 2, SUB, LANES), jnp.float32),
                pltpu.VMEM((BLOCK, SUB * cells, LANES), jnp.float32),
                pltpu.VMEM((nblk, groups, BLOCK, cells, SUB * LANES), jnp.float32),
                pltpu.SemaphoreType.DMA((nblk, groups)),
            ],
            input_output_aliases=aliases,
            compiler_params=pltpu.CompilerParams(vmem_limit_bytes=36 * 2**20),
            cost_estimate=cost(operands[1 : 1 + max(w[0] for w in where.values())], nblk, 1.0 if early is None else 0.5),
            name=name,
        )(*operands)

    image = None
    for stage, (count, blocks) in enumerate(NEAR):
        operands, where = layout(count)
        image = lags("lags_%d" % stage, image, blocks, operands, where, None, [])
    operands, early = layout(len(pieces) - 1)
    partial = pl.pallas_call(
        functools.partial(part_kernel, cells, FAR, early),
        in_specs=[VMEM] * len(operands),
        out_specs=VMEM,
        out_shape=jax.ShapeDtypeStruct((len(FAR), BLOCK, cells + 2, tiles, LANES), jnp.float32),
        compiler_params=pltpu.CompilerParams(vmem_limit_bytes=36 * 2**20),
        cost_estimate=cost(operands, len(FAR), 0.7),
        name="partial",
    )(*operands)
    operands, where = layout(len(pieces))
    return lags("lags_far", image, FAR, operands, where, set(early), [partial, rim_lo, rim_hi])


def solution(mesh):
    placed = (P(("shots", "gx"), None, None, None), P(("shots", "gx"), None, None, None))
    return jax.shard_map(
        on_device,
        mesh=mesh,
        in_specs=placed,
        out_specs=P(None, ("shots", "gx"), None),
        check_vma=False,
    )
```

```python
import functools

import jax
import jax.numpy as jnp
from jax import lax
from jax.experimental import pallas as pl
from jax.experimental.pallas import tpu as pltpu
from jax.sharding import PartitionSpec as P

Z = 64
HALF = 16
LAGS = 33
BLOCK = 3
LANES = 128
SUB = 16
SPAN = 3
RATE = 50

CHUNKS = ((16, 2, 1), (5, 4, 3), (8, 7, 6), (15, 14, 13, 12, 11, 10, 9))
BUNDLES = ((0, 1), (2,))
NEAR = (5, 4, 6, 3, 7)
FAR = (2, 8, 1, 9, 0, 10)
ALL = NEAR + FAR
SCOPED = 14 * 2**20

VMEM = pl.BlockSpec(memory_space=pltpu.VMEM)
ANY = pl.BlockSpec(memory_space=pl.ANY)


SMEM = pl.BlockSpec(memory_space=pltpu.SMEM)


def pack_kernel(rows, order_ref, s_ref, r_ref, out_ref, flip):
    _, parts, freqs, width = s_ref.shape
    for row in range(rows):
        src_row = jnp.where(order_ref[0] == 1, row, rows - 1 - row)
        for field, src in enumerate((s_ref, r_ref)):
            for p in range(parts):
                for g in range(width // (SUB * LANES)):
                    slot = flip.at[(field * parts + p) * 2 + g % 2]
                    for t in range(SUB):
                        c = (g * SUB + t) * LANES
                        slot[pl.ds(t, freqs, SUB), :] = src[src_row, p, :, c : c + LANES].astype(
                            jnp.float32
                        )
                    for f in range(freqs):
                        out_ref[row, field, p * freqs + f, g * SUB : (g + 1) * SUB] = slot[
                            f * SUB : (f + 1) * SUB
                        ].astype(jnp.bfloat16)


def pack(straight, rows, steps, source, receiver, places, weight, name):
    _, parts, freqs, width = source.shape
    tiles = width // LANES

    def spec(base):
        return pl.BlockSpec(
            (rows, parts, freqs, width),
            lambda i, order: (base + places[2] * jnp.where(order[0] == 1, i, steps - 1 - i), 0, 0, 0),
        )

    return pl.pallas_call(
        functools.partial(pack_kernel, rows),
        grid_spec=pltpu.PrefetchScalarGridSpec(
            num_scalar_prefetch=1,
            grid=(steps,),
            in_specs=[spec(places[0]), spec(places[1])],
            out_specs=pl.BlockSpec(
                (rows, 2, parts * freqs, tiles, LANES), lambda i, order: (i, 0, 0, 0, 0)
            ),
            scratch_shapes=[pltpu.VMEM((4 * parts, SUB * freqs, LANES), jnp.float32)],
        ),
        out_shape=jax.ShapeDtypeStruct(
            (rows * steps, 2, parts * freqs, tiles, LANES), jnp.bfloat16
        ),
        cost_estimate=pl.CostEstimate(
            flops=weight * 8 * rows * steps * parts * freqs * width,
            bytes_accessed=8 * rows * steps * parts * freqs * width,
            transcendentals=0,
        ),
        name=name,
    )(straight, source, receiver)


def first_kernel(core_ref, s_ref, r_ref, out_ref):
    out_ref[0, 0] = s_ref[0]
    out_ref[0, 1] = r_ref[0]


def first_rows(core, forward_field, adjoint_field):
    cells, parts, freqs, width = forward_field.shape
    rows = [cells - i for i in CHUNKS[0]]

    def at(i, core):
        row = jnp.int32(rows[0])
        for k in range(1, len(rows)):
            row = jnp.where(i == k, rows[k], row)
        return (jnp.where(core[0] == 1, row, cells - 1 - row), 0, 0, 0)

    spec = pl.BlockSpec((1, parts, freqs, width), at)
    return pl.pallas_call(
        first_kernel,
        grid_spec=pltpu.PrefetchScalarGridSpec(
            num_scalar_prefetch=1,
            grid=(len(rows),),
            in_specs=[spec, spec],
            out_specs=pl.BlockSpec(
                (1, 2, parts, freqs, width), lambda i, core: (i, 0, 0, 0, 0)
            ),
        ),
        out_shape=jax.ShapeDtypeStruct((len(rows), 2, parts, freqs, width), jnp.bfloat16),
        name="first",
    )(core, forward_field, adjoint_field)


def rim_kernel(cells, where, *refs):
    ins, (lo_ref, hi_ref) = refs[:-2], refs[-2:]

    def tile(g, _):
        at = pl.ds(pl.multiple_of(g * SUB, SUB), SUB)

        def dot(a, b):
            (s_in, s), (r_in, r) = where[a], where[b]
            total = jnp.zeros((SUB, LANES), jnp.float32)
            for k in range(ins[0].shape[2]):
                total += ins[s_in][s, 0, k, at].astype(jnp.float32) * ins[r_in][
                    r, 1, k, at
                ].astype(jnp.float32)
            return total

        for ref, x in ((lo_ref, 0), (hi_ref, cells - 1)):
            ref[0, at] = dot(x - HALF, x + HALF)
            ref[1, at] = dot(x + HALF, x - HALF)
        return 0

    lax.fori_loop(0, ins[0].shape[3] // SUB, tile, 0)


def sum_pairs(ins, where, lags, pairs, k_count, at, init):
    pairs = sorted(pairs, key=lambda p: (p[1] // SPAN, p[1] - lags[p[0]], p[1]))

    def step(k, accs):
        got = {}

        def row(field, a):
            if (field, a) not in got:
                n_in, src = where[a]
                got[field, a] = ins[n_in][src, field, k, at].astype(jnp.float32)
            return got[field, a]

        return tuple(
            acc + row(0, x - lags[t]) * row(1, x + lags[t]) for acc, (t, x) in zip(accs, pairs)
        )

    accs = lax.fori_loop(0, k_count, step, tuple(init(*p) for p in pairs), unroll=k_count)
    return zip(pairs, accs)


def blocks_of(cells, lags, keep):
    spans = []
    for x0 in range(-1, cells + 1, SPAN):
        pairs = [
            (t, x)
            for t in range(BLOCK)
            for x in range(x0, x0 + SPAN)
            if (abs(lags[t]) < HALF or 0 <= x < cells) and keep(x - lags[t], x + lags[t])
        ]
        if spans and len(spans[-1]) + len(pairs) <= BLOCK * SPAN:
            spans[-1] += pairs
        elif pairs:
            spans.append(pairs)
    return spans


def part_kernel(cells, blocks, where, done, *refs):
    ins, out_ref = refs[:-1], refs[-1]
    terms, tiles = ins[0].shape[2], ins[0].shape[3]
    zero = jnp.zeros((SUB, LANES), jnp.float32)

    def keep(a, b):
        return a in where and b in where and not (a in done and b in done)

    def tile(g, _):
        at = pl.ds(pl.multiple_of(g * SUB, SUB), SUB)
        for n, blk in enumerate(blocks):
            lags = [blk * BLOCK + t - HALF for t in range(BLOCK)]
            for pairs in blocks_of(cells, lags, keep):
                for (t, x), acc in sum_pairs(
                    ins, where, lags, pairs, terms, at, lambda t, x: zero
                ):
                    out_ref[n, t, x + 1, at] = acc
        return 0

    lax.fori_loop(0, tiles // SUB, tile, 0)


def lag_kernel(cells, blocks, where, stages, rim, aliased, *refs):
    refs = list(refs)
    core = refs.pop(0)[0]
    ins = [refs.pop(0) for _ in range(1 + max(w[0] for w in where.values()))]
    partials = [refs.pop(0) for _ in stages]
    rims = [refs.pop(0) for _ in range(2)] if rim else None
    if aliased:
        refs.pop(0)
    out_ref, sums, flip, ready, sems = refs
    terms, tiles = ins[0].shape[2], ins[0].shape[3]
    lane = lax.broadcasted_iota(jnp.int32, (SUB, LANES), 1) % Z
    first = lane == 0
    last = lane == Z - 1
    zero = jnp.zeros((SUB, LANES), jnp.float32)
    straight = core == 1

    def copies(n, g):
        cols = pl.ds(pl.multiple_of(g * (SUB * LANES), SUB * LANES), SUB * LANES)
        low = jnp.where(straight, blocks[n] * BLOCK, LAGS - (blocks[n] + 1) * BLOCK)
        return pltpu.make_async_copy(
            ready.at[n, g], out_ref.at[pl.ds(low, BLOCK), :, cols], sems.at[n, g]
        )

    def keep(a, b):
        return not any(a in rows and b in rows for rows, _ in stages)

    def tile(g, _):
        at = pl.ds(pl.multiple_of(g * SUB, SUB), SUB)
        for n, blk in enumerate(blocks):
            lags = [blk * BLOCK + t - HALF for t in range(BLOCK)]
            for pairs in blocks_of(cells, lags, keep):
                for (t, x), acc in sum_pairs(
                    ins, where, lags, pairs, terms, at, lambda t, x: zero
                ):
                    sums[t, x + 1] = acc

            def value(t, x):
                if abs(lags[t]) == HALF and not 0 <= x < cells:
                    return rims[int(x > 0)][int(lags[t] > 0), at]
                for ref, (rows, order) in zip(partials, stages):
                    if x - lags[t] in rows and x + lags[t] in rows:
                        return ref[order.index(blk), t, x + 1, at]
                return sums[t, x + 1]

            for t in range(BLOCK):
                for x in range(cells):
                    mid = value(t, x)
                    down = jnp.where(first, 0.0, pltpu.roll(mid, 1, 1))
                    up = jnp.where(last, 0.0, pltpu.roll(mid, LANES - 1, 1))
                    around = (value(t, x - 1) + value(t, x + 1)) + (down + up)
                    to = jnp.where(straight, x, cells - 1 - x)
                    flip[t, pl.ds(to, SUB, cells), :] = 0.25 * (around - 4.0 * mid)
                lag = jnp.where(straight, t, BLOCK - 1 - t)
                for c in range(SUB):
                    ready[n, g, lag, :, c * LANES : (c + 1) * LANES] = flip[
                        t, c * cells : (c + 1) * cells
                    ]
            copies(n, g).start()
        return 0

    groups = tiles // SUB
    lax.fori_loop(0, groups, tile, 0)
    for n in range(len(blocks)):
        for g in range(groups):
            copies(n, g).wait()


def exchange(peers):
    up = [(i, i + 1) for i in range(1, peers - 1, 2)]
    return up, [(j, i) for i, j in up]


def routes(peers, chunk):
    up, down = exchange(peers)
    if peers != 16 or chunk > 2:
        return up + down, ()
    steps = peers // 4
    far_up = range(0, steps - 1 - chunk)
    far_down = range(chunk, steps - 1)
    up = [p for p in up if p not in [(4 * z + 3, 4 * z + 4) for z in far_up]]
    up += [(4 * z + 3, 4 * z) for z in far_up]
    down = [p for p in down if p not in [(4 * z + 4, 4 * z + 3) for z in far_down]]
    down += [(4 * z + 4, 4 * z + 7) for z in far_down]
    swap = {4 * z for z in far_up} | {4 * z + 4 for z in far_up}
    swap |= {4 * z + 7 for z in far_down} | {4 * z + 3 for z in far_down}
    return up + down, sorted(swap)


def is_one_of(me, devices):
    found = jnp.bool_(False)
    for d in devices:
        found |= me == d
    return found


def on_device(forward_field, adjoint_field):
    cells, parts, freqs, width = forward_field.shape
    terms, tiles = parts * freqs, width // LANES
    peers = lax.axis_size("gx")
    me = lax.axis_index("gx")
    core = (me % 2).astype(jnp.int32).reshape(1)
    cores = [(i, i + 1) for i in range(0, peers, 2)] + [(i + 1, i) for i in range(0, peers, 2)]
    links = sum(exchange(peers), [])
    row_bytes = 2 * terms * width * 2

    def spans_of(rows):
        spans = []
        for r in rows:
            if spans and spans[-1][1] == r:
                spans[-1][1] = r + 1
            else:
                spans.append([r, r + 1])
        return spans

    def cut(field, rows):
        return [lax.slice_in_dim(field, a, b, axis=0) for a, b in spans_of(rows)]

    n = len(CHUNKS[0])
    raw = first_rows(core, forward_field, adjoint_field)
    raw, forward_field, adjoint_field = lax.optimization_barrier(
        (raw, forward_field, adjoint_field)
    )
    raw = lax.ppermute(raw, "gx", routes(peers, 0)[0]).reshape(2 * n, parts, freqs, width)
    own = pack(core, 2, cells // 2, forward_field, adjoint_field, (0, 0, 1), RATE, "pack")
    arrived = [None]
    for g, chunk in enumerate(CHUNKS[1:], 1):
        sent = jnp.concatenate(cut(own, [cells - i for i in chunk]), axis=0)
        if g == 2:
            sent, raw, swap = lax.optimization_barrier((sent, raw, own))
        arrived.append(lax.ppermute(sent, "gx", routes(peers, g)[0]))
    arrived[0] = pack(jnp.ones_like(core), 1, n, raw, raw, (0, 1, 2), RATE, "pack_first")
    beside = lax.ppermute(swap, "gx", cores)

    pieces = []

    def layout(count):
        operands = [own, beside]
        where = {a: (0, a) for a in range(cells)}
        where.update({-1 - a: (1, a) for a in range(cells)})
        for bundle, got in pieces[:count]:
            order = [i for g in bundle for i in CHUNKS[g]]
            where.update({cells - 1 + i: (len(operands), k) for k, i in enumerate(order)})
            operands.append(got)
        return operands, where

    def count(blocks, keep):
        total = 0
        for blk in blocks:
            lags = [blk * BLOCK + t - HALF for t in range(BLOCK)]
            total += sum(len(pairs) for pairs in blocks_of(cells, lags, keep))
        return total

    def cost(pairs, lags):
        return pl.CostEstimate(
            flops=RATE * (2 * pairs * terms * width + 20 * lags * cells * width),
            bytes_accessed=lags * cells * width * 4,
            transcendentals=0,
        )

    groups = tiles // SUB

    def partial(name, pieces_in, blocks, done):
        operands, where = layout(pieces_in)
        pairs = count(
            blocks, lambda a, b: a in where and b in where and not (a in done and b in done)
        )
        out = pl.pallas_call(
            functools.partial(part_kernel, cells, blocks, where, done),
            in_specs=[VMEM] * len(operands),
            out_specs=VMEM,
            out_shape=jax.ShapeDtypeStruct(
                (len(blocks), BLOCK, cells + 2, tiles, LANES), jnp.float32
            ),
            compiler_params=pltpu.CompilerParams(vmem_limit_bytes=SCOPED),
            cost_estimate=cost(pairs, 0),
            name=name,
        )(*operands)
        return out, (set(where), blocks)

    inner, inner_stage = partial("inner", 0, ALL, ())

    for bundle in BUNDLES:
        got = jnp.concatenate([arrived[g] for g in bundle], axis=0) if len(bundle) > 1 else arrived[bundle[0]]
        if bundle[0] == 0:
            got, inner = lax.optimization_barrier((got, inner))
        if peers == 16:
            steps = peers // 4
            hop = [(4 * z, 4 * z + 4) for z in range(steps - 1)]
            hop += [(4 * z + 7, 4 * z + 3) for z in range(steps - 1)]
            relayed = lax.ppermute(got, "gx", hop)
            swapped = jnp.concatenate(
                [
                    jnp.broadcast_to(is_one_of(me, routes(peers, g)[1]), (len(CHUNKS[g]),))
                    for g in bundle
                ]
            )
            got = jnp.where(swapped[:, None, None, None, None], relayed, got)
        pieces.append((bundle, got))
    for g in range(1 + BUNDLES[-1][-1], len(CHUNKS)):
        pieces.append(((g,), arrived[g]))

    operands, where = layout(1)
    lo, hi = pl.pallas_call(
        functools.partial(rim_kernel, cells, where),
        in_specs=[VMEM] * len(operands),
        out_specs=[VMEM, VMEM],
        out_shape=[jax.ShapeDtypeStruct((2, tiles, LANES), jnp.float32)] * 2,
        cost_estimate=pl.CostEstimate(
            flops=RATE * 8 * terms * width, bytes_accessed=6 * row_bytes, transcendentals=0
        ),
        name="rim",
    )(*operands)
    rim_lo = lax.ppermute(lo, "gx", cores)
    rim_hi = lax.ppermute(hi, "gx", links)

    def lags(name, image, pieces_in, blocks, partials, stages, rims):
        operands, where = layout(pieces_in)
        operands = [core] + operands + partials + rims
        specs = [SMEM] + [VMEM] * (len(operands) - 1)
        aliases = {}
        if image is not None:
            aliases = {len(operands): 0}
            operands.append(image)
            specs.append(ANY)
        nblk = len(blocks)
        pairs = count(
            blocks, lambda a, b: not any(a in rows and b in rows for rows, _ in stages)
        )
        return pl.pallas_call(
            functools.partial(
                lag_kernel, cells, blocks, where, stages, bool(rims), image is not None
            ),
            in_specs=specs,
            out_specs=ANY,
            out_shape=jax.ShapeDtypeStruct((LAGS, cells, width), jnp.float32),
            scratch_shapes=[
                pltpu.VMEM((BLOCK, cells + 2, SUB, LANES), jnp.float32),
                pltpu.VMEM((BLOCK, SUB * cells, LANES), jnp.float32),
                pltpu.VMEM((nblk, groups, BLOCK, cells, SUB * LANES), jnp.float32),
                pltpu.SemaphoreType.DMA((nblk, groups)),
            ],
            input_output_aliases=aliases,
            compiler_params=pltpu.CompilerParams(vmem_limit_bytes=SCOPED),
            cost_estimate=cost(pairs, BLOCK * nblk),
            name=name,
        )(*operands)

    image = lags("near", None, len(pieces) - 1, NEAR, [inner], [inner_stage], [])
    middle, middle_stage = partial("middle", len(pieces) - 1, FAR, inner_stage[0])
    return lags(
        "far",
        image,
        len(pieces),
        FAR,
        [inner, middle],
        [inner_stage, middle_stage],
        [rim_lo, rim_hi],
    )


def solution(mesh):
    placed = (P(("shots", "gx"), None, None, None), P(("shots", "gx"), None, None, None))
    return jax.shard_map(
        on_device,
        mesh=mesh,
        in_specs=placed,
        out_specs=P(None, ("shots", "gx"), None),
        check_vma=False,
    )
```

```python
import functools

import jax
import jax.numpy as jnp
from jax import lax
from jax.experimental import pallas as pl
from jax.experimental.pallas import tpu as pltpu
from jax.sharding import PartitionSpec as P

Z = 64
HALF = 16
LAGS = 33
BLOCK = 3
LANES = 128
SUB = 16
SPAN = 3
RATE = 50

CHUNKS = ((16, 4, 3, 2, 1), (11, 10, 9, 8, 7, 6, 5), (15, 14, 13, 12))
NEAR = (5, 4, 6, 3, 7, 2, 8)
FAR = (1, 9, 0, 10)
SCOPED = 14 * 2**20

VMEM = pl.BlockSpec(memory_space=pltpu.VMEM)
ANY = pl.BlockSpec(memory_space=pl.ANY)


SMEM = pl.BlockSpec(memory_space=pltpu.SMEM)


def pack_kernel(rows, order_ref, s_ref, r_ref, out_ref, flip):
    _, parts, freqs, width = s_ref.shape
    for row in range(rows):
        src_row = jnp.where(order_ref[0] == 1, row, rows - 1 - row)
        for field, src in enumerate((s_ref, r_ref)):
            for p in range(parts):
                for g in range(width // (SUB * LANES)):
                    slot = flip.at[(field * parts + p) * 2 + g % 2]
                    for t in range(SUB):
                        c = (g * SUB + t) * LANES
                        slot[pl.ds(t, freqs, SUB), :] = src[src_row, p, :, c : c + LANES].astype(
                            jnp.float32
                        )
                    for f in range(freqs):
                        out_ref[row, field, p * freqs + f, g * SUB : (g + 1) * SUB] = slot[
                            f * SUB : (f + 1) * SUB
                        ].astype(jnp.bfloat16)


def pack(straight, rows, steps, source, receiver, places, weight, name):
    _, parts, freqs, width = source.shape
    tiles = width // LANES

    def spec(base):
        return pl.BlockSpec(
            (rows, parts, freqs, width),
            lambda i, order: (base + places[2] * jnp.where(order[0] == 1, i, steps - 1 - i), 0, 0, 0),
        )

    return pl.pallas_call(
        functools.partial(pack_kernel, rows),
        grid_spec=pltpu.PrefetchScalarGridSpec(
            num_scalar_prefetch=1,
            grid=(steps,),
            in_specs=[spec(places[0]), spec(places[1])],
            out_specs=pl.BlockSpec(
                (rows, 2, parts * freqs, tiles, LANES), lambda i, order: (i, 0, 0, 0, 0)
            ),
            scratch_shapes=[pltpu.VMEM((4 * parts, SUB * freqs, LANES), jnp.float32)],
        ),
        out_shape=jax.ShapeDtypeStruct(
            (rows * steps, 2, parts * freqs, tiles, LANES), jnp.bfloat16
        ),
        cost_estimate=pl.CostEstimate(
            flops=weight * 8 * rows * steps * parts * freqs * width,
            bytes_accessed=8 * rows * steps * parts * freqs * width,
            transcendentals=0,
        ),
        name=name,
    )(straight, source, receiver)


def first_kernel(core_ref, s_ref, r_ref, out_ref):
    out_ref[0, 0] = s_ref[0]
    out_ref[0, 1] = r_ref[0]


def first_rows(core, forward_field, adjoint_field):
    cells, parts, freqs, width = forward_field.shape
    rows = [cells - i for i in CHUNKS[0]]

    def at(i, core):
        row = jnp.int32(rows[0])
        for k in range(1, len(rows)):
            row = jnp.where(i == k, rows[k], row)
        return (jnp.where(core[0] == 1, row, cells - 1 - row), 0, 0, 0)

    spec = pl.BlockSpec((1, parts, freqs, width), at)
    return pl.pallas_call(
        first_kernel,
        grid_spec=pltpu.PrefetchScalarGridSpec(
            num_scalar_prefetch=1,
            grid=(len(rows),),
            in_specs=[spec, spec],
            out_specs=pl.BlockSpec(
                (1, 2, parts, freqs, width), lambda i, core: (i, 0, 0, 0, 0)
            ),
        ),
        out_shape=jax.ShapeDtypeStruct((len(rows), 2, parts, freqs, width), jnp.bfloat16),
        name="first",
    )(core, forward_field, adjoint_field)


def rim_kernel(cells, where, *refs):
    ins, (lo_ref, hi_ref) = refs[:-2], refs[-2:]

    def tile(g, _):
        at = pl.ds(pl.multiple_of(g * SUB, SUB), SUB)

        def dot(a, b):
            (s_in, s), (r_in, r) = where[a], where[b]
            total = jnp.zeros((SUB, LANES), jnp.float32)
            for k in range(ins[0].shape[2]):
                total += ins[s_in][s, 0, k, at].astype(jnp.float32) * ins[r_in][
                    r, 1, k, at
                ].astype(jnp.float32)
            return total

        for ref, x in ((lo_ref, 0), (hi_ref, cells - 1)):
            ref[0, at] = dot(x - HALF, x + HALF)
            ref[1, at] = dot(x + HALF, x - HALF)
        return 0

    lax.fori_loop(0, ins[0].shape[3] // SUB, tile, 0)


def sum_pairs(ins, where, lags, pairs, k_count, at, init):
    pairs = sorted(pairs, key=lambda p: (p[1] // SPAN, p[1] - lags[p[0]], p[1]))

    def step(k, accs):
        got = {}

        def row(field, a):
            if (field, a) not in got:
                n_in, src = where[a]
                got[field, a] = ins[n_in][src, field, k, at].astype(jnp.float32)
            return got[field, a]

        return tuple(
            acc + row(0, x - lags[t]) * row(1, x + lags[t]) for acc, (t, x) in zip(accs, pairs)
        )

    accs = lax.fori_loop(0, k_count, step, tuple(init(*p) for p in pairs), unroll=k_count)
    return zip(pairs, accs)


def blocks_of(cells, lags, keep):
    spans = []
    for x0 in range(-1, cells + 1, SPAN):
        pairs = [
            (t, x)
            for t in range(BLOCK)
            for x in range(x0, x0 + SPAN)
            if (abs(lags[t]) < HALF or 0 <= x < cells) and keep(x - lags[t], x + lags[t])
        ]
        if spans and len(spans[-1]) + len(pairs) <= BLOCK * SPAN:
            spans[-1] += pairs
        elif pairs:
            spans.append(pairs)
    return spans


def part_kernel(cells, blocks, where, done, *refs):
    ins, out_ref = refs[:-1], refs[-1]
    terms, tiles = ins[0].shape[2], ins[0].shape[3]
    zero = jnp.zeros((SUB, LANES), jnp.float32)

    def keep(a, b):
        return a in where and b in where and not (a in done and b in done)

    def tile(g, _):
        at = pl.ds(pl.multiple_of(g * SUB, SUB), SUB)
        for n, blk in enumerate(blocks):
            lags = [blk * BLOCK + t - HALF for t in range(BLOCK)]
            for pairs in blocks_of(cells, lags, keep):
                for (t, x), acc in sum_pairs(
                    ins, where, lags, pairs, terms, at, lambda t, x: zero
                ):
                    out_ref[n, t, x + 1, at] = acc
        return 0

    lax.fori_loop(0, tiles // SUB, tile, 0)


def lag_kernel(cells, blocks, where, stages, rim, aliased, *refs):
    refs = list(refs)
    core = refs.pop(0)[0]
    ins = [refs.pop(0) for _ in range(1 + max(w[0] for w in where.values()))]
    partials = [refs.pop(0) for _ in stages]
    rims = [refs.pop(0) for _ in range(2)] if rim else None
    if aliased:
        refs.pop(0)
    out_ref, sums, flip, ready, sems = refs
    terms, tiles = ins[0].shape[2], ins[0].shape[3]
    lane = lax.broadcasted_iota(jnp.int32, (SUB, LANES), 1) % Z
    first = lane == 0
    last = lane == Z - 1
    zero = jnp.zeros((SUB, LANES), jnp.float32)
    straight = core == 1

    def copies(n, g):
        cols = pl.ds(pl.multiple_of(g * (SUB * LANES), SUB * LANES), SUB * LANES)
        low = jnp.where(straight, blocks[n] * BLOCK, LAGS - (blocks[n] + 1) * BLOCK)
        return pltpu.make_async_copy(
            ready.at[n, g], out_ref.at[pl.ds(low, BLOCK), :, cols], sems.at[n, g]
        )

    def keep(a, b):
        return not any(a in rows and b in rows for rows, _ in stages)

    def tile(g, _):
        at = pl.ds(pl.multiple_of(g * SUB, SUB), SUB)
        for n, blk in enumerate(blocks):
            lags = [blk * BLOCK + t - HALF for t in range(BLOCK)]
            for pairs in blocks_of(cells, lags, keep):
                for (t, x), acc in sum_pairs(
                    ins, where, lags, pairs, terms, at, lambda t, x: zero
                ):
                    sums[t, x + 1] = acc

            def value(t, x):
                if abs(lags[t]) == HALF and not 0 <= x < cells:
                    return rims[int(x > 0)][int(lags[t] > 0), at]
                for ref, (rows, order) in zip(partials, stages):
                    if x - lags[t] in rows and x + lags[t] in rows:
                        return ref[order.index(blk), t, x + 1, at]
                return sums[t, x + 1]

            for t in range(BLOCK):
                for x in range(cells):
                    mid = value(t, x)
                    down = jnp.where(first, 0.0, pltpu.roll(mid, 1, 1))
                    up = jnp.where(last, 0.0, pltpu.roll(mid, LANES - 1, 1))
                    around = (value(t, x - 1) + value(t, x + 1)) + (down + up)
                    to = jnp.where(straight, x, cells - 1 - x)
                    flip[t, pl.ds(to, SUB, cells), :] = 0.25 * (around - 4.0 * mid)
                lag = jnp.where(straight, t, BLOCK - 1 - t)
                for c in range(SUB):
                    ready[n, g, lag, :, c * LANES : (c + 1) * LANES] = flip[
                        t, c * cells : (c + 1) * cells
                    ]
            copies(n, g).start()
        return 0

    groups = tiles // SUB
    lax.fori_loop(0, groups, tile, 0)
    for n in range(len(blocks)):
        for g in range(groups):
            copies(n, g).wait()


def exchange(peers):
    up = [(i, i + 1) for i in range(1, peers - 1, 2)]
    return up, [(j, i) for i, j in up]


def on_device(forward_field, adjoint_field):
    cells, parts, freqs, width = forward_field.shape
    terms, tiles = parts * freqs, width // LANES
    peers = lax.axis_size("gx")
    me = lax.axis_index("gx")
    core = (me % 2).astype(jnp.int32).reshape(1)
    cores = [(i, i + 1) for i in range(0, peers, 2)] + [(i + 1, i) for i in range(0, peers, 2)]
    links = sum(exchange(peers), [])
    row_bytes = 2 * terms * width * 2

    def spans_of(rows):
        spans = []
        for r in rows:
            if spans and spans[-1][1] == r:
                spans[-1][1] = r + 1
            else:
                spans.append([r, r + 1])
        return spans

    def cut(field, rows):
        return [lax.slice_in_dim(field, a, b, axis=0) for a, b in spans_of(rows)]

    n = len(CHUNKS[0])
    raw = first_rows(core, forward_field, adjoint_field)
    raw, forward_field, adjoint_field = lax.optimization_barrier(
        (raw, forward_field, adjoint_field)
    )
    raw = lax.ppermute(raw, "gx", links).reshape(2 * n, parts, freqs, width)
    own = pack(core, 2, cells // 2, forward_field, adjoint_field, (0, 0, 1), RATE, "pack")
    arrived = [None]
    for g, chunk in enumerate(CHUNKS[1:], 1):
        sent = jnp.concatenate(cut(own, [cells - i for i in chunk]), axis=0)
        arrived.append(lax.ppermute(sent, "gx", links))
    swap, raw = lax.optimization_barrier((own, raw))
    arrived[0] = pack(jnp.ones_like(core), 1, n, raw, raw, (0, 1, 2), RATE, "pack_first")
    beside = lax.ppermute(swap, "gx", cores)

    def layout(count):
        operands = [own, beside]
        where = {a: (0, a) for a in range(cells)}
        where.update({-1 - a: (1, a) for a in range(cells)})
        for chunk, got in zip(CHUNKS[:count], arrived):
            where.update({cells - 1 + i: (len(operands), k) for k, i in enumerate(chunk)})
            operands.append(got)
        return operands, where

    def count(blocks, keep):
        total = 0
        for blk in blocks:
            lags = [blk * BLOCK + t - HALF for t in range(BLOCK)]
            total += sum(len(pairs) for pairs in blocks_of(cells, lags, keep))
        return total

    def cost(pairs, lags):
        return pl.CostEstimate(
            flops=RATE * (2 * pairs * terms * width + 20 * lags * cells * width),
            bytes_accessed=lags * cells * width * 4,
            transcendentals=0,
        )

    groups = tiles // SUB

    def partial(name, pieces_in, blocks, done):
        operands, where = layout(pieces_in)
        pairs = count(
            blocks, lambda a, b: a in where and b in where and not (a in done and b in done)
        )
        out = pl.pallas_call(
            functools.partial(part_kernel, cells, blocks, where, done),
            in_specs=[VMEM] * len(operands),
            out_specs=VMEM,
            out_shape=jax.ShapeDtypeStruct(
                (len(blocks), BLOCK, cells + 2, tiles, LANES), jnp.float32
            ),
            compiler_params=pltpu.CompilerParams(vmem_limit_bytes=SCOPED),
            cost_estimate=cost(pairs, 0),
            name=name,
        )(*operands)
        return out, (set(where), blocks)

    operands, where = layout(1)
    lo, hi = pl.pallas_call(
        functools.partial(rim_kernel, cells, where),
        in_specs=[VMEM] * len(operands),
        out_specs=[VMEM, VMEM],
        out_shape=[jax.ShapeDtypeStruct((2, tiles, LANES), jnp.float32)] * 2,
        cost_estimate=pl.CostEstimate(
            flops=RATE * 8 * terms * width, bytes_accessed=6 * row_bytes, transcendentals=0
        ),
        name="rim",
    )(*operands)
    rim_lo = lax.ppermute(lo, "gx", cores)
    rim_hi = lax.ppermute(hi, "gx", links)

    def lags(name, image, pieces_in, blocks, partials, stages, rims):
        operands, where = layout(pieces_in)
        operands = [core] + operands + partials + rims
        specs = [SMEM] + [VMEM] * (len(operands) - 1)
        aliases = {}
        if image is not None:
            aliases = {len(operands): 0}
            operands.append(image)
            specs.append(ANY)
        nblk = len(blocks)
        pairs = count(
            blocks, lambda a, b: not any(a in rows and b in rows for rows, _ in stages)
        )
        return pl.pallas_call(
            functools.partial(
                lag_kernel, cells, blocks, where, stages, bool(rims), image is not None
            ),
            in_specs=specs,
            out_specs=ANY,
            out_shape=jax.ShapeDtypeStruct((LAGS, cells, width), jnp.float32),
            scratch_shapes=[
                pltpu.VMEM((BLOCK, cells + 2, SUB, LANES), jnp.float32),
                pltpu.VMEM((BLOCK, SUB * cells, LANES), jnp.float32),
                pltpu.VMEM((nblk, groups, BLOCK, cells, SUB * LANES), jnp.float32),
                pltpu.SemaphoreType.DMA((nblk, groups)),
            ],
            input_output_aliases=aliases,
            compiler_params=pltpu.CompilerParams(vmem_limit_bytes=SCOPED),
            cost_estimate=cost(pairs, BLOCK * nblk),
            name=name,
        )(*operands)

    last = len(CHUNKS) - 1
    image = lags("near", None, last, NEAR, [], [], [])
    sums, stage = partial("partial", last, FAR, ())
    return lags("far", image, last + 1, FAR, [sums], [stage], [rim_lo, rim_hi])


def solution(mesh):
    placed = (P(("shots", "gx"), None, None, None), P(("shots", "gx"), None, None, None))
    return jax.shard_map(
        on_device,
        mesh=mesh,
        in_specs=placed,
        out_specs=P(None, ("shots", "gx"), None),
        check_vma=False,
    )
```

```python
import functools

import jax
import jax.numpy as jnp
from jax import lax
from jax.experimental import pallas as pl
from jax.experimental.pallas import tpu as pltpu
from jax.sharding import PartitionSpec as P

Z = 64
HALF = 16
LAGS = 33
BLOCK = 3
LANES = 128
SUB = 16
SPAN = 3
RATE = 50
PACK = 8000

CHUNKS = ((16, 4, 3, 2, 1), (11, 10, 9, 8, 7, 6, 5), (15, 14, 13, 12))
NEAR = (5, 4, 6, 3, 7, 2, 8)
FAR = (1, 9, 0, 10)
ALL = NEAR + FAR
SCOPED = 14 * 2**20

VMEM = pl.BlockSpec(memory_space=pltpu.VMEM)
ANY = pl.BlockSpec(memory_space=pl.ANY)


SMEM = pl.BlockSpec(memory_space=pltpu.SMEM)


def pack_kernel(core_ref, s_ref, r_ref, *refs):
    out_ref, flip = refs[-2:]
    _, parts, freqs, width = s_ref.shape
    for field, src in enumerate((s_ref, r_ref)):
        for p in range(parts):
            for g in range(width // (SUB * LANES)):
                slot = flip.at[(field * parts + p) * 2 + g % 2]
                for t in range(SUB):
                    c = (g * SUB + t) * LANES
                    slot[pl.ds(t, freqs, SUB), :] = src[0, p, :, c : c + LANES].astype(jnp.float32)
                for f in range(freqs):
                    out_ref[0, field, p * freqs + f, g * SUB : (g + 1) * SUB] = slot[
                        f * SUB : (f + 1) * SUB
                    ].astype(jnp.bfloat16)


def pack(core, source, receiver, chunk, earlier, name):
    cells, parts, freqs, width = source.shape
    tiles = width // LANES

    def at(i, core):
        row = jnp.int32(cells - chunk[0])
        for k in range(1, len(chunk)):
            row = jnp.where(i == k, cells - chunk[k], row)
        return (jnp.where(core[0] == 1, row, cells - 1 - row), 0, 0, 0)

    spec = pl.BlockSpec((1, parts, freqs, width), at)
    return pl.pallas_call(
        pack_kernel,
        grid_spec=pltpu.PrefetchScalarGridSpec(
            num_scalar_prefetch=1,
            grid=(len(chunk),),
            in_specs=[spec, spec] + [VMEM] * len(earlier),
            out_specs=pl.BlockSpec(
                (1, 2, parts * freqs, tiles, LANES), lambda i, core: (i, 0, 0, 0, 0)
            ),
            scratch_shapes=[pltpu.VMEM((4 * parts, SUB * freqs, LANES), jnp.float32)],
        ),
        out_shape=jax.ShapeDtypeStruct(
            (len(chunk), 2, parts * freqs, tiles, LANES), jnp.bfloat16
        ),
        cost_estimate=pl.CostEstimate(
            flops=0 if earlier else PACK * len(chunk) * parts * freqs * width,
            bytes_accessed=8 * len(chunk) * parts * freqs * width,
            transcendentals=0,
        ),
        name=name,
    )(core, source, receiver, *earlier)


def join_kernel(earlier_ref, *refs):
    ins, (out_ref, sems) = refs[:-2], refs[-2:]
    copies, at = [], 0
    for k, ref in enumerate(ins):
        n = ref.shape[0]
        copies.append(pltpu.make_async_copy(ref, out_ref.at[pl.ds(at, n)], sems.at[k]))
        at += n
    for copy in copies:
        copy.start()
    for copy in copies:
        copy.wait()


def join(pieces, earlier):
    rows = sum(p.shape[0] for p in pieces)
    return pl.pallas_call(
        join_kernel,
        in_specs=[VMEM] + [ANY] * len(pieces),
        out_specs=ANY,
        out_shape=jax.ShapeDtypeStruct((rows, *pieces[0].shape[1:]), pieces[0].dtype),
        scratch_shapes=[pltpu.SemaphoreType.DMA((len(pieces),))],
        name="join",
    )(earlier, *pieces)


def rim_kernel(cells, where, *refs):
    ins, (lo_ref, hi_ref) = refs[:-2], refs[-2:]

    def tile(g, _):
        at = pl.ds(pl.multiple_of(g * SUB, SUB), SUB)

        def dot(a, b):
            (s_in, s), (r_in, r) = where[a], where[b]
            total = jnp.zeros((SUB, LANES), jnp.float32)
            for k in range(ins[0].shape[2]):
                total += ins[s_in][s, 0, k, at].astype(jnp.float32) * ins[r_in][
                    r, 1, k, at
                ].astype(jnp.float32)
            return total

        for ref, x in ((lo_ref, 0), (hi_ref, cells - 1)):
            ref[0, at] = dot(x - HALF, x + HALF)
            ref[1, at] = dot(x + HALF, x - HALF)
        return 0

    lax.fori_loop(0, ins[0].shape[3] // SUB, tile, 0)


def sum_pairs(ins, where, lags, pairs, k_count, at, init):
    pairs = sorted(pairs, key=lambda p: (p[1] // SPAN, p[1] - lags[p[0]], p[1]))

    def step(k, accs):
        got = {}

        def row(field, a):
            if (field, a) not in got:
                n_in, src = where[a]
                got[field, a] = ins[n_in][src, field, k, at].astype(jnp.float32)
            return got[field, a]

        return tuple(
            acc + row(0, x - lags[t]) * row(1, x + lags[t]) for acc, (t, x) in zip(accs, pairs)
        )

    accs = lax.fori_loop(0, k_count, step, tuple(init(*p) for p in pairs), unroll=k_count)
    return zip(pairs, accs)


def blocks_of(cells, lags, keep):
    spans = []
    for x0 in range(-1, cells + 1, SPAN):
        pairs = [
            (t, x)
            for t in range(BLOCK)
            for x in range(x0, x0 + SPAN)
            if (abs(lags[t]) < HALF or 0 <= x < cells) and keep(x - lags[t], x + lags[t])
        ]
        if spans and len(spans[-1]) + len(pairs) <= BLOCK * SPAN:
            spans[-1] += pairs
        elif pairs:
            spans.append(pairs)
    return spans


def part_kernel(cells, blocks, where, done, *refs):
    ins, out_ref = refs[:-1], refs[-1]
    terms, tiles = ins[0].shape[2], ins[0].shape[3]
    zero = jnp.zeros((SUB, LANES), jnp.float32)

    def keep(a, b):
        return a in where and b in where and not (a in done and b in done)

    def tile(g, _):
        at = pl.ds(pl.multiple_of(g * SUB, SUB), SUB)
        for n, blk in enumerate(blocks):
            lags = [blk * BLOCK + t - HALF for t in range(BLOCK)]
            for pairs in blocks_of(cells, lags, keep):
                for (t, x), acc in sum_pairs(
                    ins, where, lags, pairs, terms, at, lambda t, x: zero
                ):
                    out_ref[n, t, x + 1, at] = acc
        return 0

    lax.fori_loop(0, tiles // SUB, tile, 0)


def lag_kernel(cells, blocks, where, stages, rim, aliased, *refs):
    refs = list(refs)
    core = refs.pop(0)[0]
    ins = [refs.pop(0) for _ in range(1 + max(w[0] for w in where.values()))]
    partials = [refs.pop(0) for _ in stages]
    rims = [refs.pop(0) for _ in range(2)] if rim else None
    if aliased:
        refs.pop(0)
    out_ref, sums, flip, ready, sems = refs
    terms, tiles = ins[0].shape[2], ins[0].shape[3]
    lane = lax.broadcasted_iota(jnp.int32, (SUB, LANES), 1) % Z
    first = lane == 0
    last = lane == Z - 1
    zero = jnp.zeros((SUB, LANES), jnp.float32)
    straight = core == 1

    def copies(n, g):
        cols = pl.ds(pl.multiple_of(g * (SUB * LANES), SUB * LANES), SUB * LANES)
        low = jnp.where(straight, blocks[n] * BLOCK, LAGS - (blocks[n] + 1) * BLOCK)
        return pltpu.make_async_copy(
            ready.at[n, g], out_ref.at[pl.ds(low, BLOCK), :, cols], sems.at[n, g]
        )

    def keep(a, b):
        return not any(a in rows and b in rows for rows, _ in stages)

    def tile(g, _):
        at = pl.ds(pl.multiple_of(g * SUB, SUB), SUB)
        for n, blk in enumerate(blocks):
            lags = [blk * BLOCK + t - HALF for t in range(BLOCK)]
            for pairs in blocks_of(cells, lags, keep):
                for (t, x), acc in sum_pairs(
                    ins, where, lags, pairs, terms, at, lambda t, x: zero
                ):
                    sums[t, x + 1] = acc

            def value(t, x):
                if abs(lags[t]) == HALF and not 0 <= x < cells:
                    return rims[int(x > 0)][int(lags[t] > 0), at]
                for ref, (rows, order) in zip(partials, stages):
                    if x - lags[t] in rows and x + lags[t] in rows:
                        return ref[order.index(blk), t, x + 1, at]
                return sums[t, x + 1]

            for t in range(BLOCK):
                for x in range(cells):
                    mid = value(t, x)
                    down = jnp.where(first, 0.0, pltpu.roll(mid, 1, 1))
                    up = jnp.where(last, 0.0, pltpu.roll(mid, LANES - 1, 1))
                    around = (value(t, x - 1) + value(t, x + 1)) + (down + up)
                    to = jnp.where(straight, x, cells - 1 - x)
                    flip[t, pl.ds(to, SUB, cells), :] = 0.25 * (around - 4.0 * mid)
                lag = jnp.where(straight, t, BLOCK - 1 - t)
                for c in range(SUB):
                    ready[n, g, lag, :, c * LANES : (c + 1) * LANES] = flip[
                        t, c * cells : (c + 1) * cells
                    ]
            copies(n, g).start()
        return 0

    groups = tiles // SUB
    lax.fori_loop(0, groups, tile, 0)
    for n in range(len(blocks)):
        for g in range(groups):
            copies(n, g).wait()


def exchange(peers):
    up = [(i, i + 1) for i in range(1, peers - 1, 2)]
    return up, [(j, i) for i, j in up]


def on_device(forward_field, adjoint_field):
    cells, parts, freqs, width = forward_field.shape
    terms, tiles = parts * freqs, width // LANES
    peers = lax.axis_size("gx")
    me = lax.axis_index("gx")
    core = (me % 2).astype(jnp.int32).reshape(1)
    cores = [(i, i + 1) for i in range(0, peers, 2)] + [(i + 1, i) for i in range(0, peers, 2)]
    links = sum(exchange(peers), [])
    row_bytes = 2 * terms * width * 2

    own = []
    arrived = []
    for g, chunk in enumerate(CHUNKS):
        own.append(pack(core, forward_field, adjoint_field, chunk, [], "pack_%d" % g))
        arrived.append(lax.ppermute(own[g], "gx", links))
    beside = lax.ppermute(join(own, arrived[0][0, 0, 0]), "gx", cores)

    def layout(count):
        operands = own + [beside]
        where = {}
        order = [i for chunk in CHUNKS for i in chunk]
        for g, chunk in enumerate(CHUNKS):
            where.update({cells - i: (g, k) for k, i in enumerate(chunk)})
        where.update({i - cells - 1: (len(own), k) for k, i in enumerate(order)})
        for chunk, got in zip(CHUNKS[:count], arrived):
            where.update({cells - 1 + i: (len(operands), k) for k, i in enumerate(chunk)})
            operands.append(got)
        return operands, where

    def count(blocks, keep):
        total = 0
        for blk in blocks:
            lags = [blk * BLOCK + t - HALF for t in range(BLOCK)]
            total += sum(len(pairs) for pairs in blocks_of(cells, lags, keep))
        return total

    def cost(pairs, lags):
        return pl.CostEstimate(
            flops=RATE * (2 * pairs * terms * width + 20 * lags * cells * width),
            bytes_accessed=lags * cells * width * 4,
            transcendentals=0,
        )

    groups = tiles // SUB

    def partial(name, pieces_in, blocks, done):
        operands, where = layout(pieces_in)
        pairs = count(
            blocks, lambda a, b: a in where and b in where and not (a in done and b in done)
        )
        out = pl.pallas_call(
            functools.partial(part_kernel, cells, blocks, where, done),
            in_specs=[VMEM] * len(operands),
            out_specs=VMEM,
            out_shape=jax.ShapeDtypeStruct(
                (len(blocks), BLOCK, cells + 2, tiles, LANES), jnp.float32
            ),
            compiler_params=pltpu.CompilerParams(vmem_limit_bytes=SCOPED),
            cost_estimate=cost(pairs if done else 0, 0),
            name=name,
        )(*operands)
        return out, (set(where), blocks)

    operands, where = layout(1)
    lo, hi = pl.pallas_call(
        functools.partial(rim_kernel, cells, where),
        in_specs=[VMEM] * len(operands),
        out_specs=[VMEM, VMEM],
        out_shape=[jax.ShapeDtypeStruct((2, tiles, LANES), jnp.float32)] * 2,
        cost_estimate=pl.CostEstimate(
            flops=0, bytes_accessed=0, transcendentals=0
        ),
        name="rim",
    )(*operands)
    rim_lo = lax.ppermute(lo, "gx", cores)
    rim_hi = lax.ppermute(hi, "gx", links)

    def lags(name, image, pieces_in, blocks, partials, stages, rims):
        operands, where = layout(pieces_in)
        operands = [core] + operands + partials + rims
        specs = [SMEM] + [VMEM] * (len(operands) - 1)
        aliases = {}
        if image is not None:
            aliases = {len(operands): 0}
            operands.append(image)
            specs.append(ANY)
        nblk = len(blocks)
        pairs = count(
            blocks, lambda a, b: not any(a in rows and b in rows for rows, _ in stages)
        )
        return pl.pallas_call(
            functools.partial(
                lag_kernel, cells, blocks, where, stages, bool(rims), image is not None
            ),
            in_specs=specs,
            out_specs=ANY,
            out_shape=jax.ShapeDtypeStruct((LAGS, cells, width), jnp.float32),
            scratch_shapes=[
                pltpu.VMEM((BLOCK, cells + 2, SUB, LANES), jnp.float32),
                pltpu.VMEM((BLOCK, SUB * cells, LANES), jnp.float32),
                pltpu.VMEM((nblk, groups, BLOCK, cells, SUB * LANES), jnp.float32),
                pltpu.SemaphoreType.DMA((nblk, groups)),
            ],
            input_output_aliases=aliases,
            compiler_params=pltpu.CompilerParams(vmem_limit_bytes=SCOPED),
            cost_estimate=cost(pairs, BLOCK * nblk),
            name=name,
        )(*operands)

    inner, first = partial("inner", 1, ALL, ())
    image = lags("near", None, 2, NEAR, [inner], [first], [])
    middle, second = partial("middle", 2, FAR, first[0])
    return lags("far", image, 3, FAR, [inner, middle], [first, second], [rim_lo, rim_hi])


def solution(mesh):
    placed = (P(("shots", "gx"), None, None, None), P(("shots", "gx"), None, None, None))
    return jax.shard_map(
        on_device,
        mesh=mesh,
        in_specs=placed,
        out_specs=P(None, ("shots", "gx"), None),
        check_vma=False,
    )
```

```python
import functools

import jax
import jax.numpy as jnp
from jax import lax
from jax.experimental import pallas as pl
from jax.experimental.pallas import tpu as pltpu
from jax.sharding import PartitionSpec as P

Z = 64
HALF = 16
LAGS = 33
BLOCK = 3
LANES = 128
SUB = 16
SPAN = 3
RATE = 50
PACK = 8000

CHUNKS = ((16, 15, 4, 3, 2, 1), (12, 11, 10, 9, 8, 7, 6, 5), (14, 13))
NEAR = (5, 4, 6, 3, 7, 2, 8)
FAR = (1, 9, 0, 10)
ALL = NEAR + FAR
SCOPED = 12 * 2**20
SMALL = 6 * 2**20

VMEM = pl.BlockSpec(memory_space=pltpu.VMEM)
ANY = pl.BlockSpec(memory_space=pl.ANY)


SMEM = pl.BlockSpec(memory_space=pltpu.SMEM)


def pack_kernel(core_ref, s_ref, r_ref, out_ref, flip):
    rows, parts, freqs, width = s_ref.shape
    for row in range(rows):
        src_row = jnp.where(core_ref[0] == 1, row, rows - 1 - row)
        for field, src in enumerate((s_ref, r_ref)):
            for p in range(parts):
                for g in range(width // (SUB * LANES)):
                    slot = flip.at[(field * parts + p) * 2 + g % 2]
                    for t in range(SUB):
                        c = (g * SUB + t) * LANES
                        slot[pl.ds(t, freqs, SUB), :] = src[src_row, p, :, c : c + LANES].astype(
                            jnp.float32
                        )
                    for f in range(freqs):
                        out_ref[row, field, p * freqs + f, g * SUB : (g + 1) * SUB] = slot[
                            f * SUB : (f + 1) * SUB
                        ].astype(jnp.bfloat16)


def pack(core, source, receiver, chunk, name):
    cells, parts, freqs, width = source.shape
    tiles = width // LANES
    pairs = [(cells - i) // 2 for i in chunk[::2]]

    def at(i, core):
        pair = jnp.int32(pairs[0])
        for k in range(1, len(pairs)):
            pair = jnp.where(i == k, pairs[k], pair)
        return (jnp.where(core[0] == 1, pair, cells // 2 - 1 - pair), 0, 0, 0)

    spec = pl.BlockSpec((2, parts, freqs, width), at)
    return pl.pallas_call(
        pack_kernel,
        grid_spec=pltpu.PrefetchScalarGridSpec(
            num_scalar_prefetch=1,
            grid=(len(pairs),),
            in_specs=[spec, spec],
            out_specs=pl.BlockSpec(
                (2, 2, parts * freqs, tiles, LANES), lambda i, core: (i, 0, 0, 0, 0)
            ),
            scratch_shapes=[pltpu.VMEM((4 * parts, SUB * freqs, LANES), jnp.float32)],
        ),
        out_shape=jax.ShapeDtypeStruct(
            (len(chunk), 2, parts * freqs, tiles, LANES), jnp.bfloat16
        ),
        cost_estimate=pl.CostEstimate(
            flops=PACK * len(chunk) * parts * freqs * width,
            bytes_accessed=8 * len(chunk) * parts * freqs * width,
            transcendentals=0,
        ),
        compiler_params=pltpu.CompilerParams(vmem_limit_bytes=SMALL),
        name=name,
    )(core, source, receiver)


def held_kernel(earlier_ref, in_ref, out_ref):
    def row(k, _):
        out_ref[k] = in_ref[k]
        return 0

    lax.fori_loop(0, in_ref.shape[0], row, 0)


def held(value, earlier):
    return pl.pallas_call(
        held_kernel,
        in_specs=[VMEM, VMEM],
        out_specs=VMEM,
        out_shape=jax.ShapeDtypeStruct(value.shape, value.dtype),
        compiler_params=pltpu.CompilerParams(vmem_limit_bytes=SMALL),
        name="held",
    )(earlier, value)


def rim_kernel(cells, where, *refs):
    ins, (lo_ref, hi_ref) = refs[:-2], refs[-2:]

    def tile(g, _):
        at = pl.ds(pl.multiple_of(g * SUB, SUB), SUB)

        def dot(a, b):
            (s_in, s), (r_in, r) = where[a], where[b]
            total = jnp.zeros((SUB, LANES), jnp.float32)
            for k in range(ins[0].shape[2]):
                total += ins[s_in][s, 0, k, at].astype(jnp.float32) * ins[r_in][
                    r, 1, k, at
                ].astype(jnp.float32)
            return total

        for ref, x in ((lo_ref, 0), (hi_ref, cells - 1)):
            ref[0, at] = dot(x - HALF, x + HALF)
            ref[1, at] = dot(x + HALF, x - HALF)
        return 0

    lax.fori_loop(0, ins[0].shape[3] // SUB, tile, 0)


def sum_pairs(ins, where, lags, pairs, k_count, at, init):
    pairs = sorted(pairs, key=lambda p: (p[1] // SPAN, p[1] - lags[p[0]], p[1]))

    def step(k, accs):
        got = {}

        def row(field, a):
            if (field, a) not in got:
                n_in, src = where[a]
                got[field, a] = ins[n_in][src, field, k, at].astype(jnp.float32)
            return got[field, a]

        return tuple(
            acc + row(0, x - lags[t]) * row(1, x + lags[t]) for acc, (t, x) in zip(accs, pairs)
        )

    accs = lax.fori_loop(0, k_count, step, tuple(init(*p) for p in pairs), unroll=k_count)
    return zip(pairs, accs)


def blocks_of(cells, lags, keep):
    spans = []
    for x0 in range(-1, cells + 1, SPAN):
        pairs = [
            (t, x)
            for t in range(BLOCK)
            for x in range(x0, x0 + SPAN)
            if (abs(lags[t]) < HALF or 0 <= x < cells) and keep(x - lags[t], x + lags[t])
        ]
        if spans and len(spans[-1]) + len(pairs) <= BLOCK * SPAN:
            spans[-1] += pairs
        elif pairs:
            spans.append(pairs)
    return spans


def part_kernel(cells, blocks, where, done, *refs):
    ins, out_ref = refs[:-1], refs[-1]
    terms, tiles = ins[0].shape[2], ins[0].shape[3]
    zero = jnp.zeros((SUB, LANES), jnp.float32)

    def keep(a, b):
        return a in where and b in where and not (a in done and b in done)

    def tile(g, _):
        at = pl.ds(pl.multiple_of(g * SUB, SUB), SUB)
        for n, blk in enumerate(blocks):
            lags = [blk * BLOCK + t - HALF for t in range(BLOCK)]
            for pairs in blocks_of(cells, lags, keep):
                for (t, x), acc in sum_pairs(
                    ins, where, lags, pairs, terms, at, lambda t, x: zero
                ):
                    out_ref[n, t, x + 1, at] = acc
        return 0

    lax.fori_loop(0, tiles // SUB, tile, 0)


def lag_kernel(cells, blocks, where, stages, rim, aliased, *refs):
    refs = list(refs)
    core = refs.pop(0)[0]
    ins = [refs.pop(0) for _ in range(1 + max(w[0] for w in where.values()))]
    partials = [refs.pop(0) for _ in stages]
    rims = [refs.pop(0) for _ in range(2)] if rim else None
    if aliased:
        refs.pop(0)
    out_ref, sums, flip, ready, sems = refs
    terms, tiles = ins[0].shape[2], ins[0].shape[3]
    lane = lax.broadcasted_iota(jnp.int32, (SUB, LANES), 1) % Z
    first = lane == 0
    last = lane == Z - 1
    zero = jnp.zeros((SUB, LANES), jnp.float32)
    straight = core == 1

    def copies(n, g):
        cols = pl.ds(pl.multiple_of(g * (SUB * LANES), SUB * LANES), SUB * LANES)
        low = jnp.where(straight, blocks[n] * BLOCK, LAGS - (blocks[n] + 1) * BLOCK)
        return pltpu.make_async_copy(
            ready.at[n, g], out_ref.at[pl.ds(low, BLOCK), :, cols], sems.at[n, g]
        )

    def keep(a, b):
        return not any(a in rows and b in rows for rows, _ in stages)

    def tile(g, _):
        at = pl.ds(pl.multiple_of(g * SUB, SUB), SUB)
        for n, blk in enumerate(blocks):
            lags = [blk * BLOCK + t - HALF for t in range(BLOCK)]
            for pairs in blocks_of(cells, lags, keep):
                for (t, x), acc in sum_pairs(
                    ins, where, lags, pairs, terms, at, lambda t, x: zero
                ):
                    sums[t, x + 1] = acc

            def value(t, x):
                if abs(lags[t]) == HALF and not 0 <= x < cells:
                    return rims[int(x > 0)][int(lags[t] > 0), at]
                for ref, (rows, order) in zip(partials, stages):
                    if x - lags[t] in rows and x + lags[t] in rows:
                        return ref[order.index(blk), t, x + 1, at]
                return sums[t, x + 1]

            for t in range(BLOCK):
                for x in range(cells):
                    mid = value(t, x)
                    down = jnp.where(first, 0.0, pltpu.roll(mid, 1, 1))
                    up = jnp.where(last, 0.0, pltpu.roll(mid, LANES - 1, 1))
                    around = (value(t, x - 1) + value(t, x + 1)) + (down + up)
                    to = jnp.where(straight, x, cells - 1 - x)
                    flip[t, pl.ds(to, SUB, cells), :] = 0.25 * (around - 4.0 * mid)
                lag = jnp.where(straight, t, BLOCK - 1 - t)
                for c in range(SUB):
                    ready[n, g, lag, :, c * LANES : (c + 1) * LANES] = flip[
                        t, c * cells : (c + 1) * cells
                    ]
            copies(n, g).start()
        return 0

    groups = tiles // SUB
    lax.fori_loop(0, groups, tile, 0)
    for n in range(len(blocks)):
        for g in range(groups):
            copies(n, g).wait()


def exchange(peers):
    up = [(i, i + 1) for i in range(1, peers - 1, 2)]
    return up, [(j, i) for i, j in up]


def on_device(forward_field, adjoint_field):
    cells, parts, freqs, width = forward_field.shape
    terms, tiles = parts * freqs, width // LANES
    peers = lax.axis_size("gx")
    me = lax.axis_index("gx")
    core = (me % 2).astype(jnp.int32).reshape(1)
    cores = [(i, i + 1) for i in range(0, peers, 2)] + [(i + 1, i) for i in range(0, peers, 2)]
    links = sum(exchange(peers), [])
    row_bytes = 2 * terms * width * 2

    own = []
    arrived = []
    for g, chunk in enumerate(CHUNKS):
        own.append(pack(core, forward_field, adjoint_field, chunk, "pack_%d" % g))
        sent = own[g]
        if g == 2:
            sent = held(sent, arrived[0][0, 0, 0])
        arrived.append(lax.ppermute(sent, "gx", links))
    beside = lax.ppermute(jnp.concatenate(own, axis=0), "gx", cores)

    def layout(count):
        operands = own + [beside]
        where = {}
        order = [i for chunk in CHUNKS for i in chunk]
        for g, chunk in enumerate(CHUNKS):
            where.update({cells - i: (g, k) for k, i in enumerate(chunk)})
        where.update({i - cells - 1: (len(own), k) for k, i in enumerate(order)})
        for chunk, got in zip(CHUNKS[:count], arrived):
            where.update({cells - 1 + i: (len(operands), k) for k, i in enumerate(chunk)})
            operands.append(got)
        return operands, where

    def count(blocks, keep):
        total = 0
        for blk in blocks:
            lags = [blk * BLOCK + t - HALF for t in range(BLOCK)]
            total += sum(len(pairs) for pairs in blocks_of(cells, lags, keep))
        return total

    def cost(pairs, lags):
        return pl.CostEstimate(
            flops=RATE * (2 * pairs * terms * width + 20 * lags * cells * width),
            bytes_accessed=lags * cells * width * 4,
            transcendentals=0,
        )

    groups = tiles // SUB

    def partial(name, pieces_in, blocks, done):
        operands, where = layout(pieces_in)
        pairs = count(
            blocks, lambda a, b: a in where and b in where and not (a in done and b in done)
        )
        out = pl.pallas_call(
            functools.partial(part_kernel, cells, blocks, where, done),
            in_specs=[VMEM] * len(operands),
            out_specs=VMEM,
            out_shape=jax.ShapeDtypeStruct(
                (len(blocks), BLOCK, cells + 2, tiles, LANES), jnp.float32
            ),
            compiler_params=pltpu.CompilerParams(vmem_limit_bytes=SCOPED),
            cost_estimate=cost(pairs if done else 0, 0),
            name=name,
        )(*operands)
        return out, (set(where), blocks)

    operands, where = layout(1)
    lo, hi = pl.pallas_call(
        functools.partial(rim_kernel, cells, where),
        in_specs=[VMEM] * len(operands),
        out_specs=[VMEM, VMEM],
        out_shape=[jax.ShapeDtypeStruct((2, tiles, LANES), jnp.float32)] * 2,
        cost_estimate=pl.CostEstimate(
            flops=0, bytes_accessed=0, transcendentals=0
        ),
        compiler_params=pltpu.CompilerParams(vmem_limit_bytes=SMALL),
        name="rim",
    )(*operands)
    rim_lo = lax.ppermute(lo, "gx", cores)
    rim_hi = lax.ppermute(hi, "gx", links)

    def lags(name, image, pieces_in, blocks, partials, stages, rims):
        operands, where = layout(pieces_in)
        operands = [core] + operands + partials + rims
        specs = [SMEM] + [VMEM] * (len(operands) - 1)
        aliases = {}
        if image is not None:
            aliases = {len(operands): 0}
            operands.append(image)
            specs.append(ANY)
        nblk = len(blocks)
        pairs = count(
            blocks, lambda a, b: not any(a in rows and b in rows for rows, _ in stages)
        )
        return pl.pallas_call(
            functools.partial(
                lag_kernel, cells, blocks, where, stages, bool(rims), image is not None
            ),
            in_specs=specs,
            out_specs=ANY,
            out_shape=jax.ShapeDtypeStruct((LAGS, cells, width), jnp.float32),
            scratch_shapes=[
                pltpu.VMEM((BLOCK, cells + 2, SUB, LANES), jnp.float32),
                pltpu.VMEM((BLOCK, SUB * cells, LANES), jnp.float32),
                pltpu.VMEM((nblk, groups, BLOCK, cells, SUB * LANES), jnp.float32),
                pltpu.SemaphoreType.DMA((nblk, groups)),
            ],
            input_output_aliases=aliases,
            compiler_params=pltpu.CompilerParams(vmem_limit_bytes=SCOPED),
            cost_estimate=cost(pairs, BLOCK * nblk),
            name=name,
        )(*operands)

    inner, first = partial("inner", 1, ALL, ())
    image = lags("near", None, 2, NEAR, [inner], [first], [])
    middle, second = partial("middle", 2, FAR, first[0])
    return lags("far", image, 3, FAR, [inner, middle], [first, second], [rim_lo, rim_hi])


def solution(mesh):
    placed = (P(("shots", "gx"), None, None, None), P(("shots", "gx"), None, None, None))
    return jax.shard_map(
        on_device,
        mesh=mesh,
        in_specs=placed,
        out_specs=P(None, ("shots", "gx"), None),
        check_vma=False,
    )
```

```python
import functools

import jax
import jax.numpy as jnp
from jax import lax
from jax.experimental import pallas as pl
from jax.experimental.pallas import tpu as pltpu
from jax.sharding import PartitionSpec as P

Z = 64
HALF = 16
LAGS = 33
BLOCK = 3
LANES = 128
SUB = 16
SPAN = 3
RATE = 50
PACK = 8000

CHUNKS = ((16, 4, 3, 2, 1), (11, 10, 9, 8, 7, 6, 5), (15, 14, 13, 12))
NEAR = (5, 4, 6, 3, 7, 2, 8)
FAR = (1, 9, 0, 10)
ALL = NEAR + FAR
SCOPED = 12 * 2**20
SMALL = 6 * 2**20
LARGE = 48 * 2**20

VMEM = pl.BlockSpec(memory_space=pltpu.VMEM)
ANY = pl.BlockSpec(memory_space=pl.ANY)


SMEM = pl.BlockSpec(memory_space=pltpu.SMEM)


def pack_kernel(core_ref, s_ref, r_ref, *refs):
    outs, (whole_ref, inbox, flip, sems) = refs[:-4], refs[-4:]
    cells, parts, freqs, width = s_ref.shape
    order = [cells - i for chunk in CHUNKS for i in chunk]

    def copy(k, field, row):
        src = (s_ref, r_ref)[field]
        return pltpu.make_async_copy(src.at[row], inbox.at[k, field], sems.at[k, field])

    for k, row in enumerate(order):
        for field in (0, 1):
            copy(k, field, jnp.where(core_ref[0] == 1, row, cells - 1 - row)).start()
    base = 0
    for out_ref in outs:

        def one(n, _):
            k = base + n
            for field in (0, 1):
                copy(k, field, 0).wait()
                for p in range(parts):
                    for g in range(width // (SUB * LANES)):
                        slot = flip.at[(field * parts + p) * 2 + g % 2]
                        for t in range(SUB):
                            c = (g * SUB + t) * LANES
                            slot[pl.ds(t, freqs, SUB), :] = inbox[
                                k, field, p, :, c : c + LANES
                            ].astype(jnp.float32)
                        for f in range(freqs):
                            lines = slot[f * SUB : (f + 1) * SUB].astype(jnp.bfloat16)
                            at = (field, p * freqs + f, slice(g * SUB, (g + 1) * SUB))
                            out_ref[(n, *at)] = lines
                            whole_ref[(k, *at)] = lines
            return 0

        lax.fori_loop(0, out_ref.shape[0], one, 0)
        base += out_ref.shape[0]


def pack(core, source, receiver):
    cells, parts, freqs, width = source.shape
    terms, tiles = parts * freqs, width // LANES
    counts = [len(chunk) for chunk in CHUNKS] + [cells]
    hbm = pl.BlockSpec(memory_space=pltpu.HBM)
    return pl.pallas_call(
        pack_kernel,
        in_specs=[SMEM, hbm, hbm],
        out_specs=[VMEM] * len(counts),
        out_shape=[
            jax.ShapeDtypeStruct((n, 2, terms, tiles, LANES), jnp.bfloat16) for n in counts
        ],
        scratch_shapes=[
            pltpu.VMEM((cells, 2, parts, freqs, width), jnp.bfloat16),
            pltpu.VMEM((4 * parts, SUB * freqs, LANES), jnp.float32),
            pltpu.SemaphoreType.DMA((cells, 2)),
        ],
        cost_estimate=pl.CostEstimate(
            flops=PACK * cells * terms * width,
            bytes_accessed=8 * cells * terms * width,
            transcendentals=0,
        ),
        compiler_params=pltpu.CompilerParams(vmem_limit_bytes=LARGE),
        name="pack",
    )(core, source, receiver)


def held_kernel(earlier_ref, in_ref, out_ref):
    def row(k, _):
        out_ref[k] = in_ref[k]
        return 0

    lax.fori_loop(0, in_ref.shape[0], row, 0)


def held(value, earlier):
    return pl.pallas_call(
        held_kernel,
        in_specs=[VMEM, VMEM],
        out_specs=VMEM,
        out_shape=jax.ShapeDtypeStruct(value.shape, value.dtype),
        compiler_params=pltpu.CompilerParams(vmem_limit_bytes=SMALL),
        name="held",
    )(earlier, value)


def rim_kernel(cells, where, *refs):
    ins, (lo_ref, hi_ref) = refs[:-2], refs[-2:]

    def tile(g, _):
        at = pl.ds(pl.multiple_of(g * SUB, SUB), SUB)

        def dot(a, b):
            (s_in, s), (r_in, r) = where[a], where[b]
            total = jnp.zeros((SUB, LANES), jnp.float32)
            for k in range(ins[0].shape[2]):
                total += ins[s_in][s, 0, k, at].astype(jnp.float32) * ins[r_in][
                    r, 1, k, at
                ].astype(jnp.float32)
            return total

        for ref, x in ((lo_ref, 0), (hi_ref, cells - 1)):
            ref[0, at] = dot(x - HALF, x + HALF)
            ref[1, at] = dot(x + HALF, x - HALF)
        return 0

    lax.fori_loop(0, ins[0].shape[3] // SUB, tile, 0)


def sum_pairs(ins, where, lags, pairs, k_count, at, init):
    pairs = sorted(pairs, key=lambda p: (p[1] // SPAN, p[1] - lags[p[0]], p[1]))

    def step(k, accs):
        got = {}

        def row(field, a):
            if (field, a) not in got:
                n_in, src = where[a]
                got[field, a] = ins[n_in][src, field, k, at].astype(jnp.float32)
            return got[field, a]

        return tuple(
            acc + row(0, x - lags[t]) * row(1, x + lags[t]) for acc, (t, x) in zip(accs, pairs)
        )

    accs = lax.fori_loop(0, k_count, step, tuple(init(*p) for p in pairs), unroll=k_count)
    return zip(pairs, accs)


def blocks_of(cells, lags, keep):
    spans = []
    for x0 in range(-1, cells + 1, SPAN):
        pairs = [
            (t, x)
            for t in range(BLOCK)
            for x in range(x0, x0 + SPAN)
            if (abs(lags[t]) < HALF or 0 <= x < cells) and keep(x - lags[t], x + lags[t])
        ]
        if spans and len(spans[-1]) + len(pairs) <= BLOCK * SPAN:
            spans[-1] += pairs
        elif pairs:
            spans.append(pairs)
    return spans


def part_kernel(cells, blocks, where, done, *refs):
    ins, out_ref = refs[:-1], refs[-1]
    terms, tiles = ins[0].shape[2], ins[0].shape[3]
    zero = jnp.zeros((SUB, LANES), jnp.float32)

    def keep(a, b):
        return a in where and b in where and not (a in done and b in done)

    def tile(g, _):
        at = pl.ds(pl.multiple_of(g * SUB, SUB), SUB)
        for n, blk in enumerate(blocks):
            lags = [blk * BLOCK + t - HALF for t in range(BLOCK)]
            for pairs in blocks_of(cells, lags, keep):
                for (t, x), acc in sum_pairs(
                    ins, where, lags, pairs, terms, at, lambda t, x: zero
                ):
                    out_ref[n, t, x + 1, at] = acc
        return 0

    lax.fori_loop(0, tiles // SUB, tile, 0)


def lag_kernel(cells, blocks, where, stages, rim, aliased, *refs):
    refs = list(refs)
    core = refs.pop(0)[0]
    ins = [refs.pop(0) for _ in range(1 + max(w[0] for w in where.values()))]
    partials = [refs.pop(0) for _ in stages]
    rims = [refs.pop(0) for _ in range(2)] if rim else None
    if aliased:
        refs.pop(0)
    out_ref, sums, flip, ready, sems = refs
    terms, tiles = ins[0].shape[2], ins[0].shape[3]
    lane = lax.broadcasted_iota(jnp.int32, (SUB, LANES), 1) % Z
    first = lane == 0
    last = lane == Z - 1
    zero = jnp.zeros((SUB, LANES), jnp.float32)
    straight = core == 1

    def copies(n, g):
        cols = pl.ds(pl.multiple_of(g * (SUB * LANES), SUB * LANES), SUB * LANES)
        low = jnp.where(straight, blocks[n] * BLOCK, LAGS - (blocks[n] + 1) * BLOCK)
        return pltpu.make_async_copy(
            ready.at[n, g], out_ref.at[pl.ds(low, BLOCK), :, cols], sems.at[n, g]
        )

    def keep(a, b):
        return not any(a in rows and b in rows for rows, _ in stages)

    def tile(g, _):
        at = pl.ds(pl.multiple_of(g * SUB, SUB), SUB)
        for n, blk in enumerate(blocks):
            lags = [blk * BLOCK + t - HALF for t in range(BLOCK)]
            for pairs in blocks_of(cells, lags, keep):
                for (t, x), acc in sum_pairs(
                    ins, where, lags, pairs, terms, at, lambda t, x: zero
                ):
                    sums[t, x + 1] = acc

            def value(t, x):
                if abs(lags[t]) == HALF and not 0 <= x < cells:
                    return rims[int(x > 0)][int(lags[t] > 0), at]
                for ref, (rows, order) in zip(partials, stages):
                    if x - lags[t] in rows and x + lags[t] in rows:
                        return ref[order.index(blk), t, x + 1, at]
                return sums[t, x + 1]

            for t in range(BLOCK):
                for x in range(cells):
                    mid = value(t, x)
                    down = jnp.where(first, 0.0, pltpu.roll(mid, 1, 1))
                    up = jnp.where(last, 0.0, pltpu.roll(mid, LANES - 1, 1))
                    around = (value(t, x - 1) + value(t, x + 1)) + (down + up)
                    to = jnp.where(straight, x, cells - 1 - x)
                    flip[t, pl.ds(to, SUB, cells), :] = 0.25 * (around - 4.0 * mid)
                lag = jnp.where(straight, t, BLOCK - 1 - t)
                for c in range(SUB):
                    ready[n, g, lag, :, c * LANES : (c + 1) * LANES] = flip[
                        t, c * cells : (c + 1) * cells
                    ]
            copies(n, g).start()
        return 0

    groups = tiles // SUB
    lax.fori_loop(0, groups, tile, 0)
    for n in range(len(blocks)):
        for g in range(groups):
            copies(n, g).wait()


def exchange(peers):
    up = [(i, i + 1) for i in range(1, peers - 1, 2)]
    return up, [(j, i) for i, j in up]


def on_device(forward_field, adjoint_field):
    cells, parts, freqs, width = forward_field.shape
    terms, tiles = parts * freqs, width // LANES
    peers = lax.axis_size("gx")
    me = lax.axis_index("gx")
    core = (me % 2).astype(jnp.int32).reshape(1)
    cores = [(i, i + 1) for i in range(0, peers, 2)] + [(i + 1, i) for i in range(0, peers, 2)]
    links = sum(exchange(peers), [])
    row_bytes = 2 * terms * width * 2

    *own, whole = pack(core, forward_field, adjoint_field)
    arrived = []
    for g, sent in enumerate(own):
        if g == 2:
            sent = held(sent, arrived[0][0, 0, 0])
        arrived.append(lax.ppermute(sent, "gx", links))
    beside = lax.ppermute(whole, "gx", cores)

    def layout(count):
        operands = own + [beside]
        where = {}
        order = [i for chunk in CHUNKS for i in chunk]
        for g, chunk in enumerate(CHUNKS):
            where.update({cells - i: (g, k) for k, i in enumerate(chunk)})
        where.update({i - cells - 1: (len(own), k) for k, i in enumerate(order)})
        for chunk, got in zip(CHUNKS[:count], arrived):
            where.update({cells - 1 + i: (len(operands), k) for k, i in enumerate(chunk)})
            operands.append(got)
        return operands, where

    def count(blocks, keep):
        total = 0
        for blk in blocks:
            lags = [blk * BLOCK + t - HALF for t in range(BLOCK)]
            total += sum(len(pairs) for pairs in blocks_of(cells, lags, keep))
        return total

    def cost(pairs, lags):
        return pl.CostEstimate(
            flops=RATE * (2 * pairs * terms * width + 20 * lags * cells * width),
            bytes_accessed=lags * cells * width * 4,
            transcendentals=0,
        )

    groups = tiles // SUB

    def partial(name, pieces_in, blocks, done):
        operands, where = layout(pieces_in)
        pairs = count(
            blocks, lambda a, b: a in where and b in where and not (a in done and b in done)
        )
        out = pl.pallas_call(
            functools.partial(part_kernel, cells, blocks, where, done),
            in_specs=[VMEM] * len(operands),
            out_specs=VMEM,
            out_shape=jax.ShapeDtypeStruct(
                (len(blocks), BLOCK, cells + 2, tiles, LANES), jnp.float32
            ),
            compiler_params=pltpu.CompilerParams(vmem_limit_bytes=SCOPED),
            cost_estimate=cost(pairs if done else 0, 0),
            name=name,
        )(*operands)
        return out, (set(where), blocks)

    operands, where = layout(1)
    lo, hi = pl.pallas_call(
        functools.partial(rim_kernel, cells, where),
        in_specs=[VMEM] * len(operands),
        out_specs=[VMEM, VMEM],
        out_shape=[jax.ShapeDtypeStruct((2, tiles, LANES), jnp.float32)] * 2,
        cost_estimate=pl.CostEstimate(
            flops=0, bytes_accessed=0, transcendentals=0
        ),
        compiler_params=pltpu.CompilerParams(vmem_limit_bytes=SMALL),
        name="rim",
    )(*operands)
    rim_lo = lax.ppermute(lo, "gx", cores)
    rim_hi = lax.ppermute(hi, "gx", links)

    def lags(name, image, pieces_in, blocks, partials, stages, rims):
        operands, where = layout(pieces_in)
        operands = [core] + operands + partials + rims
        specs = [SMEM] + [VMEM] * (len(operands) - 1)
        aliases = {}
        if image is not None:
            aliases = {len(operands): 0}
            operands.append(image)
            specs.append(ANY)
        nblk = len(blocks)
        pairs = count(
            blocks, lambda a, b: not any(a in rows and b in rows for rows, _ in stages)
        )
        return pl.pallas_call(
            functools.partial(
                lag_kernel, cells, blocks, where, stages, bool(rims), image is not None
            ),
            in_specs=specs,
            out_specs=ANY,
            out_shape=jax.ShapeDtypeStruct((LAGS, cells, width), jnp.float32),
            scratch_shapes=[
                pltpu.VMEM((BLOCK, cells + 2, SUB, LANES), jnp.float32),
                pltpu.VMEM((BLOCK, SUB * cells, LANES), jnp.float32),
                pltpu.VMEM((nblk, groups, BLOCK, cells, SUB * LANES), jnp.float32),
                pltpu.SemaphoreType.DMA((nblk, groups)),
            ],
            input_output_aliases=aliases,
            compiler_params=pltpu.CompilerParams(vmem_limit_bytes=SCOPED),
            cost_estimate=cost(pairs, BLOCK * nblk),
            name=name,
        )(*operands)

    inner, first = partial("inner", 1, ALL, ())
    image = lags("near", None, 2, NEAR, [inner], [first], [])
    middle, second = partial("middle", 2, FAR, first[0])
    return lags("far", image, 3, FAR, [inner, middle], [first, second], [rim_lo, rim_hi])


def solution(mesh):
    placed = (P(("shots", "gx"), None, None, None), P(("shots", "gx"), None, None, None))
    return jax.shard_map(
        on_device,
        mesh=mesh,
        in_specs=placed,
        out_specs=P(None, ("shots", "gx"), None),
        check_vma=False,
    )
```

```python
import functools

import jax
import jax.numpy as jnp
from jax import lax
from jax.experimental import pallas as pl
from jax.experimental.pallas import tpu as pltpu
from jax.sharding import PartitionSpec as P

Z = 64
HALF = 16
LAGS = 33
BLOCK = 3
LANES = 128
SUB = 16
SPAN = 3
RATE = 50
PACK = 8000

CHUNKS = ((16, 1), (3, 2), (5, 4), (12, 11, 10, 9, 8, 7, 6), (15, 14, 13))
HOLD = 2
BUNDLES = ((0, 1), (2,))
NEAR = (5, 4, 6, 3, 7, 2, 8)
FAR = (1, 9, 0, 10)
ALL = NEAR + FAR
SCOPED = 12 * 2**20
SMALL = 6 * 2**20
LARGE = 48 * 2**20

VMEM = pl.BlockSpec(memory_space=pltpu.VMEM)
ANY = pl.BlockSpec(memory_space=pl.ANY)


SMEM = pl.BlockSpec(memory_space=pltpu.SMEM)


def pack_kernel(core_ref, s_ref, r_ref, *refs):
    outs, (inbox, flip, sems) = refs[:-3], refs[-3:]
    cells, parts, freqs, width = s_ref.shape
    order = [cells - i for chunk in CHUNKS for i in chunk]

    def copy(k, field, row):
        src = (s_ref, r_ref)[field]
        return pltpu.make_async_copy(src.at[row], inbox.at[k, field], sems.at[k, field])

    for k, row in enumerate(order):
        for field in (0, 1):
            copy(k, field, jnp.where(core_ref[0] == 1, row, cells - 1 - row)).start()
    base = 0
    for out_ref in outs:

        def one(n, _):
            k = base + n
            for field in (0, 1):
                copy(k, field, 0).wait()
                for p in range(parts):
                    for g in range(width // (SUB * LANES)):
                        slot = flip.at[(field * parts + p) * 2 + g % 2]
                        for t in range(SUB):
                            c = (g * SUB + t) * LANES
                            slot[pl.ds(t, freqs, SUB), :] = inbox[
                                k, field, p, :, c : c + LANES
                            ].astype(jnp.float32)
                        for f in range(freqs):
                            out_ref[n, field, p * freqs + f, g * SUB : (g + 1) * SUB] = slot[
                                f * SUB : (f + 1) * SUB
                            ].astype(jnp.bfloat16)
            return 0

        lax.fori_loop(0, out_ref.shape[0], one, 0)
        base += out_ref.shape[0]


def pack(core, source, receiver):
    cells, parts, freqs, width = source.shape
    terms, tiles = parts * freqs, width // LANES
    counts = [len(chunk) for chunk in CHUNKS]
    hbm = pl.BlockSpec(memory_space=pltpu.HBM)
    return pl.pallas_call(
        pack_kernel,
        in_specs=[SMEM, hbm, hbm],
        out_specs=[VMEM] * len(counts),
        out_shape=[
            jax.ShapeDtypeStruct((n, 2, terms, tiles, LANES), jnp.bfloat16) for n in counts
        ],
        scratch_shapes=[
            pltpu.VMEM((cells, 2, parts, freqs, width), jnp.bfloat16),
            pltpu.VMEM((4 * parts, SUB * freqs, LANES), jnp.float32),
            pltpu.SemaphoreType.DMA((cells, 2)),
        ],
        cost_estimate=pl.CostEstimate(
            flops=PACK * cells * terms * width,
            bytes_accessed=8 * cells * terms * width,
            transcendentals=0,
        ),
        compiler_params=pltpu.CompilerParams(vmem_limit_bytes=LARGE),
        name="pack",
    )(core, source, receiver)


def held_kernel(earlier_ref, in_ref, out_ref):
    def row(k, _):
        out_ref[k] = in_ref[k]
        return 0

    lax.fori_loop(0, in_ref.shape[0], row, 0)


def held(value, earlier):
    return pl.pallas_call(
        held_kernel,
        in_specs=[VMEM, VMEM],
        out_specs=VMEM,
        out_shape=jax.ShapeDtypeStruct(value.shape, value.dtype),
        compiler_params=pltpu.CompilerParams(vmem_limit_bytes=SMALL),
        name="held",
    )(earlier, value)


def rim_kernel(cells, where, *refs):
    ins, (lo_ref, hi_ref) = refs[:-2], refs[-2:]

    def tile(g, _):
        at = pl.ds(pl.multiple_of(g * SUB, SUB), SUB)

        def dot(a, b):
            (s_in, s), (r_in, r) = where[a], where[b]
            total = jnp.zeros((SUB, LANES), jnp.float32)
            for k in range(ins[0].shape[2]):
                total += ins[s_in][s, 0, k, at].astype(jnp.float32) * ins[r_in][
                    r, 1, k, at
                ].astype(jnp.float32)
            return total

        for ref, x in ((lo_ref, 0), (hi_ref, cells - 1)):
            ref[0, at] = dot(x - HALF, x + HALF)
            ref[1, at] = dot(x + HALF, x - HALF)
        return 0

    lax.fori_loop(0, ins[0].shape[3] // SUB, tile, 0)


def sum_pairs(ins, where, lags, pairs, k_count, at, init):
    pairs = sorted(pairs, key=lambda p: (p[1] // SPAN, p[1] - lags[p[0]], p[1]))

    def step(k, accs):
        got = {}

        def row(field, a):
            if (field, a) not in got:
                n_in, src = where[a]
                got[field, a] = ins[n_in][src, field, k, at].astype(jnp.float32)
            return got[field, a]

        return tuple(
            acc + row(0, x - lags[t]) * row(1, x + lags[t]) for acc, (t, x) in zip(accs, pairs)
        )

    accs = lax.fori_loop(0, k_count, step, tuple(init(*p) for p in pairs), unroll=k_count)
    return zip(pairs, accs)


def blocks_of(cells, lags, keep):
    spans = []
    for x0 in range(-1, cells + 1, SPAN):
        pairs = [
            (t, x)
            for t in range(BLOCK)
            for x in range(x0, x0 + SPAN)
            if (abs(lags[t]) < HALF or 0 <= x < cells) and keep(x - lags[t], x + lags[t])
        ]
        if spans and len(spans[-1]) + len(pairs) <= BLOCK * SPAN:
            spans[-1] += pairs
        elif pairs:
            spans.append(pairs)
    return spans


def part_kernel(cells, blocks, where, done, *refs):
    ins, out_ref = refs[:-1], refs[-1]
    terms, tiles = ins[0].shape[2], ins[0].shape[3]
    zero = jnp.zeros((SUB, LANES), jnp.float32)

    def keep(a, b):
        return a in where and b in where and not (a in done and b in done)

    def tile(g, _):
        at = pl.ds(pl.multiple_of(g * SUB, SUB), SUB)
        for n, blk in enumerate(blocks):
            lags = [blk * BLOCK + t - HALF for t in range(BLOCK)]
            for pairs in blocks_of(cells, lags, keep):
                for (t, x), acc in sum_pairs(
                    ins, where, lags, pairs, terms, at, lambda t, x: zero
                ):
                    out_ref[n, t, x + 1, at] = acc
        return 0

    lax.fori_loop(0, tiles // SUB, tile, 0)


def lag_kernel(cells, blocks, where, stages, rim, aliased, *refs):
    refs = list(refs)
    core = refs.pop(0)[0]
    ins = [refs.pop(0) for _ in range(1 + max(w[0] for w in where.values()))]
    partials = [refs.pop(0) for _ in stages]
    rims = [refs.pop(0) for _ in range(2)] if rim else None
    if aliased:
        refs.pop(0)
    out_ref, sums, flip, ready, sems = refs
    terms, tiles = ins[0].shape[2], ins[0].shape[3]
    lane = lax.broadcasted_iota(jnp.int32, (SUB, LANES), 1) % Z
    first = lane == 0
    last = lane == Z - 1
    zero = jnp.zeros((SUB, LANES), jnp.float32)
    straight = core == 1

    def copies(n, g):
        cols = pl.ds(pl.multiple_of(g * (SUB * LANES), SUB * LANES), SUB * LANES)
        low = jnp.where(straight, blocks[n] * BLOCK, LAGS - (blocks[n] + 1) * BLOCK)
        return pltpu.make_async_copy(
            ready.at[n, g], out_ref.at[pl.ds(low, BLOCK), :, cols], sems.at[n, g]
        )

    def keep(a, b):
        return not any(a in rows and b in rows for rows, _ in stages)

    def tile(g, _):
        at = pl.ds(pl.multiple_of(g * SUB, SUB), SUB)
        for n, blk in enumerate(blocks):
            lags = [blk * BLOCK + t - HALF for t in range(BLOCK)]
            for pairs in blocks_of(cells, lags, keep):
                for (t, x), acc in sum_pairs(
                    ins, where, lags, pairs, terms, at, lambda t, x: zero
                ):
                    sums[t, x + 1] = acc

            def value(t, x):
                if abs(lags[t]) == HALF and not 0 <= x < cells:
                    return rims[int(x > 0)][int(lags[t] > 0), at]
                for ref, (rows, order) in zip(partials, stages):
                    if x - lags[t] in rows and x + lags[t] in rows:
                        return ref[order.index(blk), t, x + 1, at]
                return sums[t, x + 1]

            for t in range(BLOCK):
                for x in range(cells):
                    mid = value(t, x)
                    down = jnp.where(first, 0.0, pltpu.roll(mid, 1, 1))
                    up = jnp.where(last, 0.0, pltpu.roll(mid, LANES - 1, 1))
                    around = (value(t, x - 1) + value(t, x + 1)) + (down + up)
                    to = jnp.where(straight, x, cells - 1 - x)
                    flip[t, pl.ds(to, SUB, cells), :] = 0.25 * (around - 4.0 * mid)
                lag = jnp.where(straight, t, BLOCK - 1 - t)
                for c in range(SUB):
                    ready[n, g, lag, :, c * LANES : (c + 1) * LANES] = flip[
                        t, c * cells : (c + 1) * cells
                    ]
            copies(n, g).start()
        return 0

    groups = tiles // SUB
    lax.fori_loop(0, groups, tile, 0)
    for n in range(len(blocks)):
        for g in range(groups):
            copies(n, g).wait()


def exchange(peers):
    up = [(i, i + 1) for i in range(1, peers - 1, 2)]
    return up, [(j, i) for i, j in up]


def routes(peers, chunk):
    up, down = exchange(peers)
    if peers != 16 or chunk > 2:
        return up + down, ()
    steps = peers // 4
    far_up = range(0, steps - 1 - chunk)
    far_down = range(chunk, steps - 1)
    up = [p for p in up if p not in [(4 * z + 3, 4 * z + 4) for z in far_up]]
    up += [(4 * z + 3, 4 * z) for z in far_up]
    down = [p for p in down if p not in [(4 * z + 4, 4 * z + 3) for z in far_down]]
    down += [(4 * z + 4, 4 * z + 7) for z in far_down]
    swap = {4 * z for z in far_up} | {4 * z + 4 for z in far_up}
    swap |= {4 * z + 7 for z in far_down} | {4 * z + 3 for z in far_down}
    return up + down, sorted(swap)


def is_one_of(me, devices):
    found = jnp.bool_(False)
    for d in devices:
        found |= me == d
    return found


def on_device(forward_field, adjoint_field):
    cells, parts, freqs, width = forward_field.shape
    terms, tiles = parts * freqs, width // LANES
    peers = lax.axis_size("gx")
    me = lax.axis_index("gx")
    core = (me % 2).astype(jnp.int32).reshape(1)
    cores = [(i, i + 1) for i in range(0, peers, 2)] + [(i + 1, i) for i in range(0, peers, 2)]
    links = sum(exchange(peers), [])
    row_bytes = 2 * terms * width * 2

    own = list(pack(core, forward_field, adjoint_field))
    arrived = []
    for g, sent in enumerate(own):
        if g == len(CHUNKS) - 1:
            sent = held(sent, arrived[HOLD][0, 0, 0])
        arrived.append(lax.ppermute(sent, "gx", routes(peers, g)[0]))
    beside = lax.ppermute(jnp.concatenate(own, axis=0), "gx", cores)

    pieces = []
    for bundle in BUNDLES:
        got = jnp.concatenate([arrived[g] for g in bundle], axis=0)
        if peers == 16:
            steps = peers // 4
            hop = [(4 * z, 4 * z + 4) for z in range(steps - 1)]
            hop += [(4 * z + 7, 4 * z + 3) for z in range(steps - 1)]
            relayed = lax.ppermute(got, "gx", hop)
            swapped = jnp.concatenate(
                [
                    jnp.broadcast_to(is_one_of(me, routes(peers, g)[1]), (len(CHUNKS[g]),))
                    for g in bundle
                ]
            )
            got = jnp.where(swapped[:, None, None, None, None], relayed, got)
        pieces.append((sum((CHUNKS[g] for g in bundle), ()), got))
    for g in range(1 + BUNDLES[-1][-1], len(CHUNKS)):
        pieces.append((CHUNKS[g], arrived[g]))

    def layout(count):
        operands = own + [beside]
        where = {}
        order = [i for chunk in CHUNKS for i in chunk]
        for g, chunk in enumerate(CHUNKS):
            where.update({cells - i: (g, k) for k, i in enumerate(chunk)})
        where.update({i - cells - 1: (len(own), k) for k, i in enumerate(order)})
        for chunk, got in pieces[:count]:
            where.update({cells - 1 + i: (len(operands), k) for k, i in enumerate(chunk)})
            operands.append(got)
        return operands, where

    def count(blocks, keep):
        total = 0
        for blk in blocks:
            lags = [blk * BLOCK + t - HALF for t in range(BLOCK)]
            total += sum(len(pairs) for pairs in blocks_of(cells, lags, keep))
        return total

    def cost(pairs, lags):
        return pl.CostEstimate(
            flops=RATE * (2 * pairs * terms * width + 20 * lags * cells * width),
            bytes_accessed=lags * cells * width * 4,
            transcendentals=0,
        )

    groups = tiles // SUB

    def partial(name, pieces_in, blocks, done):
        operands, where = layout(pieces_in)
        pairs = count(
            blocks, lambda a, b: a in where and b in where and not (a in done and b in done)
        )
        out = pl.pallas_call(
            functools.partial(part_kernel, cells, blocks, where, done),
            in_specs=[VMEM] * len(operands),
            out_specs=VMEM,
            out_shape=jax.ShapeDtypeStruct(
                (len(blocks), BLOCK, cells + 2, tiles, LANES), jnp.float32
            ),
            compiler_params=pltpu.CompilerParams(vmem_limit_bytes=SCOPED),
            cost_estimate=cost(pairs if done else 0, 0),
            name=name,
        )(*operands)
        return out, (set(where), blocks)

    operands, where = layout(1)
    lo, hi = pl.pallas_call(
        functools.partial(rim_kernel, cells, where),
        in_specs=[VMEM] * len(operands),
        out_specs=[VMEM, VMEM],
        out_shape=[jax.ShapeDtypeStruct((2, tiles, LANES), jnp.float32)] * 2,
        cost_estimate=pl.CostEstimate(
            flops=0, bytes_accessed=0, transcendentals=0
        ),
        compiler_params=pltpu.CompilerParams(vmem_limit_bytes=SMALL),
        name="rim",
    )(*operands)
    rim_lo = lax.ppermute(lo, "gx", cores)
    rim_hi = lax.ppermute(hi, "gx", links)

    def lags(name, image, pieces_in, blocks, partials, stages, rims):
        operands, where = layout(pieces_in)
        operands = [core] + operands + partials + rims
        specs = [SMEM] + [VMEM] * (len(operands) - 1)
        aliases = {}
        if image is not None:
            aliases = {len(operands): 0}
            operands.append(image)
            specs.append(ANY)
        nblk = len(blocks)
        pairs = count(
            blocks, lambda a, b: not any(a in rows and b in rows for rows, _ in stages)
        )
        return pl.pallas_call(
            functools.partial(
                lag_kernel, cells, blocks, where, stages, bool(rims), image is not None
            ),
            in_specs=specs,
            out_specs=ANY,
            out_shape=jax.ShapeDtypeStruct((LAGS, cells, width), jnp.float32),
            scratch_shapes=[
                pltpu.VMEM((BLOCK, cells + 2, SUB, LANES), jnp.float32),
                pltpu.VMEM((BLOCK, SUB * cells, LANES), jnp.float32),
                pltpu.VMEM((nblk, groups, BLOCK, cells, SUB * LANES), jnp.float32),
                pltpu.SemaphoreType.DMA((nblk, groups)),
            ],
            input_output_aliases=aliases,
            compiler_params=pltpu.CompilerParams(vmem_limit_bytes=SCOPED),
            cost_estimate=cost(pairs, BLOCK * nblk),
            name=name,
        )(*operands)

    inner, first = partial("inner", 2, ALL, ())
    image = lags("near", None, 3, NEAR, [inner], [first], [])
    middle, second = partial("middle", 3, FAR, first[0])
    return lags("far", image, 4, FAR, [inner, middle], [first, second], [rim_lo, rim_hi])


def solution(mesh):
    placed = (P(("shots", "gx"), None, None, None), P(("shots", "gx"), None, None, None))
    return jax.shard_map(
        on_device,
        mesh=mesh,
        in_specs=placed,
        out_specs=P(None, ("shots", "gx"), None),
        check_vma=False,
    )
```

```python
import functools

import jax
import jax.numpy as jnp
from jax import lax
from jax.experimental import pallas as pl
from jax.experimental.pallas import tpu as pltpu
from jax.sharding import PartitionSpec as P

Z = 64
HALF = 16
LAGS = 33
BLOCK = 3
LANES = 128
SUB = 16
SPAN = 3
RATE = 50
PACK = 8000

CHUNKS = ((16, 4, 3, 2, 1), (11, 10, 9, 8, 7, 6, 5), (15, 14, 13, 12))
NEAR = (5, 4, 6, 3, 7, 2, 8)
FAR = (1, 9, 0, 10)
ALL = NEAR + FAR
SCOPED = 12 * 2**20
SMALL = 6 * 2**20
LARGE = 48 * 2**20

VMEM = pl.BlockSpec(memory_space=pltpu.VMEM)
ANY = pl.BlockSpec(memory_space=pl.ANY)


SMEM = pl.BlockSpec(memory_space=pltpu.SMEM)


def pack_kernel(core_ref, s_ref, r_ref, *refs):
    outs, (whole_ref, inbox, flip, sems, sent) = refs[:-5], refs[-5:]
    cells, parts, freqs, width = s_ref.shape
    order = [cells - i for chunk in CHUNKS for i in chunk]

    def copy(k, field, row):
        src = (s_ref, r_ref)[field]
        return pltpu.make_async_copy(src.at[row], inbox.at[k, field], sems.at[k, field])

    for k, row in enumerate(order):
        for field in (0, 1):
            copy(k, field, jnp.where(core_ref[0] == 1, row, cells - 1 - row)).start()
    base = 0
    kept = []
    for out_ref in outs:

        def one(n, _):
            k = base + n
            for field in (0, 1):
                copy(k, field, 0).wait()
                for p in range(parts):
                    for g in range(width // (SUB * LANES)):
                        slot = flip.at[(field * parts + p) * 2 + g % 2]
                        for t in range(SUB):
                            c = (g * SUB + t) * LANES
                            slot[pl.ds(t, freqs, SUB), :] = inbox[
                                k, field, p, :, c : c + LANES
                            ].astype(jnp.float32)
                        for f in range(freqs):
                            out_ref[n, field, p * freqs + f, g * SUB : (g + 1) * SUB] = slot[
                                f * SUB : (f + 1) * SUB
                            ].astype(jnp.bfloat16)
            return 0

        count = out_ref.shape[0]
        lax.fori_loop(0, count, one, 0)
        kept.append(
            pltpu.make_async_copy(out_ref, whole_ref.at[pl.ds(base, count)], sent.at[len(kept)])
        )
        kept[-1].start()
        base += count
    for copied in kept:
        copied.wait()


def pack(core, source, receiver):
    cells, parts, freqs, width = source.shape
    terms, tiles = parts * freqs, width // LANES
    counts = [len(chunk) for chunk in CHUNKS] + [cells]
    hbm = pl.BlockSpec(memory_space=pltpu.HBM)
    return pl.pallas_call(
        pack_kernel,
        in_specs=[SMEM, hbm, hbm],
        out_specs=[VMEM] * len(CHUNKS) + [hbm],
        out_shape=[
            jax.ShapeDtypeStruct((n, 2, terms, tiles, LANES), jnp.bfloat16) for n in counts
        ],
        scratch_shapes=[
            pltpu.VMEM((cells, 2, parts, freqs, width), jnp.bfloat16),
            pltpu.VMEM((4 * parts, SUB * freqs, LANES), jnp.float32),
            pltpu.SemaphoreType.DMA((cells, 2)),
            pltpu.SemaphoreType.DMA((len(CHUNKS),)),
        ],
        cost_estimate=pl.CostEstimate(
            flops=PACK * cells * terms * width,
            bytes_accessed=8 * cells * terms * width,
            transcendentals=0,
        ),
        compiler_params=pltpu.CompilerParams(vmem_limit_bytes=LARGE),
        name="pack",
    )(core, source, receiver)


def held_kernel(earlier_ref, in_ref, out_ref):
    def row(k, _):
        out_ref[k] = in_ref[k]
        return 0

    lax.fori_loop(0, in_ref.shape[0], row, 0)


def held(value, earlier):
    return pl.pallas_call(
        held_kernel,
        in_specs=[VMEM, VMEM],
        out_specs=VMEM,
        out_shape=jax.ShapeDtypeStruct(value.shape, value.dtype),
        compiler_params=pltpu.CompilerParams(vmem_limit_bytes=SMALL),
        name="held",
    )(earlier, value)


def rim_kernel(cells, where, *refs):
    ins, (lo_ref, hi_ref) = refs[:-2], refs[-2:]

    def tile(g, _):
        at = pl.ds(pl.multiple_of(g * SUB, SUB), SUB)

        def dot(a, b):
            (s_in, s), (r_in, r) = where[a], where[b]
            total = jnp.zeros((SUB, LANES), jnp.float32)
            for k in range(ins[0].shape[2]):
                total += ins[s_in][s, 0, k, at].astype(jnp.float32) * ins[r_in][
                    r, 1, k, at
                ].astype(jnp.float32)
            return total

        for ref, x in ((lo_ref, 0), (hi_ref, cells - 1)):
            ref[0, at] = dot(x - HALF, x + HALF)
            ref[1, at] = dot(x + HALF, x - HALF)
        return 0

    lax.fori_loop(0, ins[0].shape[3] // SUB, tile, 0)


def sum_pairs(ins, where, lags, pairs, k_count, at, init):
    pairs = sorted(pairs, key=lambda p: (p[1] // SPAN, p[1] - lags[p[0]], p[1]))

    def step(k, accs):
        got = {}

        def row(field, a):
            if (field, a) not in got:
                n_in, src = where[a]
                got[field, a] = ins[n_in][src, field, k, at].astype(jnp.float32)
            return got[field, a]

        return tuple(
            acc + row(0, x - lags[t]) * row(1, x + lags[t]) for acc, (t, x) in zip(accs, pairs)
        )

    accs = lax.fori_loop(0, k_count, step, tuple(init(*p) for p in pairs), unroll=k_count)
    return zip(pairs, accs)


def blocks_of(cells, lags, keep):
    spans = []
    for x0 in range(-1, cells + 1, SPAN):
        pairs = [
            (t, x)
            for t in range(BLOCK)
            for x in range(x0, x0 + SPAN)
            if (abs(lags[t]) < HALF or 0 <= x < cells) and keep(x - lags[t], x + lags[t])
        ]
        if spans and len(spans[-1]) + len(pairs) <= BLOCK * SPAN:
            spans[-1] += pairs
        elif pairs:
            spans.append(pairs)
    return spans


def part_kernel(cells, blocks, where, done, *refs):
    ins, out_ref = refs[:-1], refs[-1]
    terms, tiles = ins[0].shape[2], ins[0].shape[3]
    zero = jnp.zeros((SUB, LANES), jnp.float32)

    def keep(a, b):
        return a in where and b in where and not (a in done and b in done)

    def tile(g, _):
        at = pl.ds(pl.multiple_of(g * SUB, SUB), SUB)
        for n, blk in enumerate(blocks):
            lags = [blk * BLOCK + t - HALF for t in range(BLOCK)]
            for pairs in blocks_of(cells, lags, keep):
                for (t, x), acc in sum_pairs(
                    ins, where, lags, pairs, terms, at, lambda t, x: zero
                ):
                    out_ref[n, t, x + 1, at] = acc
        return 0

    lax.fori_loop(0, tiles // SUB, tile, 0)


def lag_kernel(cells, blocks, where, stages, rim, aliased, *refs):
    refs = list(refs)
    core = refs.pop(0)[0]
    ins = [refs.pop(0) for _ in range(1 + max(w[0] for w in where.values()))]
    partials = [refs.pop(0) for _ in stages]
    rims = [refs.pop(0) for _ in range(2)] if rim else None
    if aliased:
        refs.pop(0)
    out_ref, sums, flip, ready, sems = refs
    terms, tiles = ins[0].shape[2], ins[0].shape[3]
    lane = lax.broadcasted_iota(jnp.int32, (SUB, LANES), 1) % Z
    first = lane == 0
    last = lane == Z - 1
    zero = jnp.zeros((SUB, LANES), jnp.float32)
    straight = core == 1

    def copies(n, g):
        cols = pl.ds(pl.multiple_of(g * (SUB * LANES), SUB * LANES), SUB * LANES)
        low = jnp.where(straight, blocks[n] * BLOCK, LAGS - (blocks[n] + 1) * BLOCK)
        return pltpu.make_async_copy(
            ready.at[n, g], out_ref.at[pl.ds(low, BLOCK), :, cols], sems.at[n, g]
        )

    def keep(a, b):
        return not any(a in rows and b in rows for rows, _ in stages)

    def tile(g, _):
        at = pl.ds(pl.multiple_of(g * SUB, SUB), SUB)
        for n, blk in enumerate(blocks):
            lags = [blk * BLOCK + t - HALF for t in range(BLOCK)]
            for pairs in blocks_of(cells, lags, keep):
                for (t, x), acc in sum_pairs(
                    ins, where, lags, pairs, terms, at, lambda t, x: zero
                ):
                    sums[t, x + 1] = acc

            def value(t, x):
                if abs(lags[t]) == HALF and not 0 <= x < cells:
                    return rims[int(x > 0)][int(lags[t] > 0), at]
                for ref, (rows, order) in zip(partials, stages):
                    if x - lags[t] in rows and x + lags[t] in rows:
                        return ref[order.index(blk), t, x + 1, at]
                return sums[t, x + 1]

            for t in range(BLOCK):
                for x in range(cells):
                    mid = value(t, x)
                    down = jnp.where(first, 0.0, pltpu.roll(mid, 1, 1))
                    up = jnp.where(last, 0.0, pltpu.roll(mid, LANES - 1, 1))
                    around = (value(t, x - 1) + value(t, x + 1)) + (down + up)
                    to = jnp.where(straight, x, cells - 1 - x)
                    flip[t, pl.ds(to, SUB, cells), :] = 0.25 * (around - 4.0 * mid)
                lag = jnp.where(straight, t, BLOCK - 1 - t)
                for c in range(SUB):
                    ready[n, g, lag, :, c * LANES : (c + 1) * LANES] = flip[
                        t, c * cells : (c + 1) * cells
                    ]
            copies(n, g).start()
        return 0

    groups = tiles // SUB
    lax.fori_loop(0, groups, tile, 0)
    for n in range(len(blocks)):
        for g in range(groups):
            copies(n, g).wait()


def exchange(peers):
    up = [(i, i + 1) for i in range(1, peers - 1, 2)]
    return up, [(j, i) for i, j in up]


def on_device(forward_field, adjoint_field):
    cells, parts, freqs, width = forward_field.shape
    terms, tiles = parts * freqs, width // LANES
    peers = lax.axis_size("gx")
    me = lax.axis_index("gx")
    core = (me % 2).astype(jnp.int32).reshape(1)
    cores = [(i, i + 1) for i in range(0, peers, 2)] + [(i + 1, i) for i in range(0, peers, 2)]
    links = sum(exchange(peers), [])
    row_bytes = 2 * terms * width * 2

    *own, whole = pack(core, forward_field, adjoint_field)
    arrived = []
    for g, sent in enumerate(own):
        if g == 2:
            sent = held(sent, arrived[0][0, 0, 0])
        arrived.append(lax.ppermute(sent, "gx", links))
    beside = lax.ppermute(whole, "gx", cores)

    def layout(count):
        operands = own + [beside]
        where = {}
        order = [i for chunk in CHUNKS for i in chunk]
        for g, chunk in enumerate(CHUNKS):
            where.update({cells - i: (g, k) for k, i in enumerate(chunk)})
        where.update({i - cells - 1: (len(own), k) for k, i in enumerate(order)})
        for chunk, got in zip(CHUNKS[:count], arrived):
            where.update({cells - 1 + i: (len(operands), k) for k, i in enumerate(chunk)})
            operands.append(got)
        return operands, where

    def count(blocks, keep):
        total = 0
        for blk in blocks:
            lags = [blk * BLOCK + t - HALF for t in range(BLOCK)]
            total += sum(len(pairs) for pairs in blocks_of(cells, lags, keep))
        return total

    def cost(pairs, lags):
        return pl.CostEstimate(
            flops=RATE * (2 * pairs * terms * width + 20 * lags * cells * width),
            bytes_accessed=lags * cells * width * 4,
            transcendentals=0,
        )

    groups = tiles // SUB

    def partial(name, pieces_in, blocks, done):
        operands, where = layout(pieces_in)
        pairs = count(
            blocks, lambda a, b: a in where and b in where and not (a in done and b in done)
        )
        out = pl.pallas_call(
            functools.partial(part_kernel, cells, blocks, where, done),
            in_specs=[VMEM] * len(operands),
            out_specs=VMEM,
            out_shape=jax.ShapeDtypeStruct(
                (len(blocks), BLOCK, cells + 2, tiles, LANES), jnp.float32
            ),
            compiler_params=pltpu.CompilerParams(vmem_limit_bytes=SCOPED),
            cost_estimate=cost(pairs if done else 0, 0),
            name=name,
        )(*operands)
        return out, (set(where), blocks)

    operands, where = layout(1)
    lo, hi = pl.pallas_call(
        functools.partial(rim_kernel, cells, where),
        in_specs=[VMEM] * len(operands),
        out_specs=[VMEM, VMEM],
        out_shape=[jax.ShapeDtypeStruct((2, tiles, LANES), jnp.float32)] * 2,
        cost_estimate=pl.CostEstimate(
            flops=0, bytes_accessed=0, transcendentals=0
        ),
        compiler_params=pltpu.CompilerParams(vmem_limit_bytes=SMALL),
        name="rim",
    )(*operands)
    rim_lo = lax.ppermute(lo, "gx", cores)
    rim_hi = lax.ppermute(hi, "gx", links)

    def lags(name, image, pieces_in, blocks, partials, stages, rims):
        operands, where = layout(pieces_in)
        operands = [core] + operands + partials + rims
        specs = [SMEM] + [VMEM] * (len(operands) - 1)
        aliases = {}
        if image is not None:
            aliases = {len(operands): 0}
            operands.append(image)
            specs.append(ANY)
        nblk = len(blocks)
        pairs = count(
            blocks, lambda a, b: not any(a in rows and b in rows for rows, _ in stages)
        )
        return pl.pallas_call(
            functools.partial(
                lag_kernel, cells, blocks, where, stages, bool(rims), image is not None
            ),
            in_specs=specs,
            out_specs=ANY,
            out_shape=jax.ShapeDtypeStruct((LAGS, cells, width), jnp.float32),
            scratch_shapes=[
                pltpu.VMEM((BLOCK, cells + 2, SUB, LANES), jnp.float32),
                pltpu.VMEM((BLOCK, SUB * cells, LANES), jnp.float32),
                pltpu.VMEM((nblk, groups, BLOCK, cells, SUB * LANES), jnp.float32),
                pltpu.SemaphoreType.DMA((nblk, groups)),
            ],
            input_output_aliases=aliases,
            compiler_params=pltpu.CompilerParams(vmem_limit_bytes=SCOPED),
            cost_estimate=cost(pairs, BLOCK * nblk),
            name=name,
        )(*operands)

    inner, first = partial("inner", 1, ALL, ())
    image = lags("near", None, 2, NEAR, [inner], [first], [])
    middle, second = partial("middle", 2, FAR, first[0])
    return lags("far", image, 3, FAR, [inner, middle], [first, second], [rim_lo, rim_hi])


def solution(mesh):
    placed = (P(("shots", "gx"), None, None, None), P(("shots", "gx"), None, None, None))
    return jax.shard_map(
        on_device,
        mesh=mesh,
        in_specs=placed,
        out_specs=P(None, ("shots", "gx"), None),
        check_vma=False,
    )
```

```python
import functools

import jax
import jax.numpy as jnp
from jax import lax
from jax.experimental import pallas as pl
from jax.experimental.pallas import tpu as pltpu
from jax.sharding import PartitionSpec as P

Z = 64
HALF = 16
LAGS = 33
BLOCK = 3
LANES = 128
SUB = 16
SPAN = 3
RATE = 50
PACK = 8000

CHUNKS = ((16, 4, 3, 2, 1), (11, 10, 9, 8, 7, 6, 5), (15, 14, 13, 12))
NEAR = (5, 4, 6, 3, 7, 2, 8)
FAR = (1, 9, 0, 10)
ALL = NEAR + FAR
SCOPED = 12 * 2**20
SMALL = 6 * 2**20
LARGE = 48 * 2**20

VMEM = pl.BlockSpec(memory_space=pltpu.VMEM)
ANY = pl.BlockSpec(memory_space=pl.ANY)


SMEM = pl.BlockSpec(memory_space=pltpu.SMEM)


def pack_kernel(core_ref, s_ref, r_ref, *refs):
    outs, (whole_ref, inbox, flip, sems, sent) = refs[:-5], refs[-5:]
    cells, parts, freqs, width = s_ref.shape
    order = [cells - i for chunk in CHUNKS for i in chunk]

    def copy(k, field, row):
        src = (s_ref, r_ref)[field]
        return pltpu.make_async_copy(src.at[row], inbox.at[k, field], sems.at[k, field])

    for k, row in enumerate(order):
        for field in (0, 1):
            copy(k, field, jnp.where(core_ref[0] == 1, row, cells - 1 - row)).start()
    base = 0
    kept = []
    for out_ref in outs:

        def one(n, _):
            k = base + n
            for field in (0, 1):
                copy(k, field, 0).wait()
                for p in range(parts):
                    for g in range(width // (SUB * LANES)):
                        slot = flip.at[(field * parts + p) * 2 + g % 2]
                        for t in range(SUB):
                            c = (g * SUB + t) * LANES
                            slot[pl.ds(t, freqs, SUB), :] = inbox[
                                k, field, p, :, c : c + LANES
                            ].astype(jnp.float32)
                        for f in range(freqs):
                            out_ref[n, field, p * freqs + f, g * SUB : (g + 1) * SUB] = slot[
                                f * SUB : (f + 1) * SUB
                            ].astype(jnp.bfloat16)
            return 0

        count = out_ref.shape[0]
        lax.fori_loop(0, count, one, 0, unroll=count)
        kept.append(
            pltpu.make_async_copy(out_ref, whole_ref.at[pl.ds(base, count)], sent.at[len(kept)])
        )
        kept[-1].start()
        base += count
    for copied in kept:
        copied.wait()


def pack(core, source, receiver):
    cells, parts, freqs, width = source.shape
    terms, tiles = parts * freqs, width // LANES
    counts = [len(chunk) for chunk in CHUNKS] + [cells]
    hbm = pl.BlockSpec(memory_space=pltpu.HBM)
    return pl.pallas_call(
        pack_kernel,
        in_specs=[SMEM, hbm, hbm],
        out_specs=[VMEM] * len(CHUNKS) + [hbm],
        out_shape=[
            jax.ShapeDtypeStruct((n, 2, terms, tiles, LANES), jnp.bfloat16) for n in counts
        ],
        scratch_shapes=[
            pltpu.VMEM((cells, 2, parts, freqs, width), jnp.bfloat16),
            pltpu.VMEM((4 * parts, SUB * freqs, LANES), jnp.float32),
            pltpu.SemaphoreType.DMA((cells, 2)),
            pltpu.SemaphoreType.DMA((len(CHUNKS),)),
        ],
        cost_estimate=pl.CostEstimate(
            flops=PACK * cells * terms * width,
            bytes_accessed=8 * cells * terms * width,
            transcendentals=0,
        ),
        compiler_params=pltpu.CompilerParams(vmem_limit_bytes=LARGE),
        name="pack",
    )(core, source, receiver)


def held_kernel(earlier_ref, in_ref, out_ref):
    def row(k, _):
        out_ref[k] = in_ref[k]
        return 0

    lax.fori_loop(0, in_ref.shape[0], row, 0)


def held(value, earlier):
    return pl.pallas_call(
        held_kernel,
        in_specs=[VMEM, VMEM],
        out_specs=VMEM,
        out_shape=jax.ShapeDtypeStruct(value.shape, value.dtype),
        compiler_params=pltpu.CompilerParams(vmem_limit_bytes=SMALL),
        name="held",
    )(earlier, value)


def rim_kernel(cells, where, *refs):
    ins, (lo_ref, hi_ref) = refs[:-2], refs[-2:]

    def tile(g, _):
        at = pl.ds(pl.multiple_of(g * SUB, SUB), SUB)

        def dot(a, b):
            (s_in, s), (r_in, r) = where[a], where[b]
            total = jnp.zeros((SUB, LANES), jnp.float32)
            for k in range(ins[0].shape[2]):
                total += ins[s_in][s, 0, k, at].astype(jnp.float32) * ins[r_in][
                    r, 1, k, at
                ].astype(jnp.float32)
            return total

        for ref, x in ((lo_ref, 0), (hi_ref, cells - 1)):
            ref[0, at] = dot(x - HALF, x + HALF)
            ref[1, at] = dot(x + HALF, x - HALF)
        return 0

    lax.fori_loop(0, ins[0].shape[3] // SUB, tile, 0)


def sum_pairs(ins, where, lags, pairs, k_count, at, init):
    pairs = sorted(pairs, key=lambda p: (p[1] // SPAN, p[1] - lags[p[0]], p[1]))

    def step(k, accs):
        got = {}

        def row(field, a):
            if (field, a) not in got:
                n_in, src = where[a]
                got[field, a] = ins[n_in][src, field, k, at].astype(jnp.float32)
            return got[field, a]

        return tuple(
            acc + row(0, x - lags[t]) * row(1, x + lags[t]) for acc, (t, x) in zip(accs, pairs)
        )

    accs = lax.fori_loop(0, k_count, step, tuple(init(*p) for p in pairs), unroll=k_count)
    return zip(pairs, accs)


def blocks_of(cells, lags, keep):
    spans = []
    for x0 in range(-1, cells + 1, SPAN):
        pairs = [
            (t, x)
            for t in range(BLOCK)
            for x in range(x0, x0 + SPAN)
            if (abs(lags[t]) < HALF or 0 <= x < cells) and keep(x - lags[t], x + lags[t])
        ]
        if spans and len(spans[-1]) + len(pairs) <= BLOCK * SPAN:
            spans[-1] += pairs
        elif pairs:
            spans.append(pairs)
    return spans


def part_kernel(cells, blocks, where, done, *refs):
    ins, out_ref = refs[:-1], refs[-1]
    terms, tiles = ins[0].shape[2], ins[0].shape[3]
    zero = jnp.zeros((SUB, LANES), jnp.float32)

    def keep(a, b):
        return a in where and b in where and not (a in done and b in done)

    def tile(g, _):
        at = pl.ds(pl.multiple_of(g * SUB, SUB), SUB)
        for n, blk in enumerate(blocks):
            lags = [blk * BLOCK + t - HALF for t in range(BLOCK)]
            for pairs in blocks_of(cells, lags, keep):
                for (t, x), acc in sum_pairs(
                    ins, where, lags, pairs, terms, at, lambda t, x: zero
                ):
                    out_ref[n, t, x + 1, at] = acc
        return 0

    lax.fori_loop(0, tiles // SUB, tile, 0)


def lag_kernel(cells, blocks, where, stages, rim, aliased, *refs):
    refs = list(refs)
    core = refs.pop(0)[0]
    ins = [refs.pop(0) for _ in range(1 + max(w[0] for w in where.values()))]
    partials = [refs.pop(0) for _ in stages]
    rims = [refs.pop(0) for _ in range(2)] if rim else None
    if aliased:
        refs.pop(0)
    out_ref, sums, flip, ready, sems = refs
    terms, tiles = ins[0].shape[2], ins[0].shape[3]
    lane = lax.broadcasted_iota(jnp.int32, (SUB, LANES), 1) % Z
    first = lane == 0
    last = lane == Z - 1
    zero = jnp.zeros((SUB, LANES), jnp.float32)
    straight = core == 1

    def copies(n, g):
        cols = pl.ds(pl.multiple_of(g * (SUB * LANES), SUB * LANES), SUB * LANES)
        low = jnp.where(straight, blocks[n] * BLOCK, LAGS - (blocks[n] + 1) * BLOCK)
        return pltpu.make_async_copy(
            ready.at[n, g], out_ref.at[pl.ds(low, BLOCK), :, cols], sems.at[n, g]
        )

    def keep(a, b):
        return not any(a in rows and b in rows for rows, _ in stages)

    def tile(g, _):
        at = pl.ds(pl.multiple_of(g * SUB, SUB), SUB)
        for n, blk in enumerate(blocks):
            lags = [blk * BLOCK + t - HALF for t in range(BLOCK)]
            for pairs in blocks_of(cells, lags, keep):
                for (t, x), acc in sum_pairs(
                    ins, where, lags, pairs, terms, at, lambda t, x: zero
                ):
                    sums[t, x + 1] = acc

            def value(t, x):
                if abs(lags[t]) == HALF and not 0 <= x < cells:
                    return rims[int(x > 0)][int(lags[t] > 0), at]
                for ref, (rows, order) in zip(partials, stages):
                    if x - lags[t] in rows and x + lags[t] in rows:
                        return ref[order.index(blk), t, x + 1, at]
                return sums[t, x + 1]

            for t in range(BLOCK):
                for x in range(cells):
                    mid = value(t, x)
                    down = jnp.where(first, 0.0, pltpu.roll(mid, 1, 1))
                    up = jnp.where(last, 0.0, pltpu.roll(mid, LANES - 1, 1))
                    around = (value(t, x - 1) + value(t, x + 1)) + (down + up)
                    to = jnp.where(straight, x, cells - 1 - x)
                    flip[t, pl.ds(to, SUB, cells), :] = 0.25 * (around - 4.0 * mid)
                lag = jnp.where(straight, t, BLOCK - 1 - t)
                for c in range(SUB):
                    ready[n, g, lag, :, c * LANES : (c + 1) * LANES] = flip[
                        t, c * cells : (c + 1) * cells
                    ]
            copies(n, g).start()
        return 0

    groups = tiles // SUB
    lax.fori_loop(0, groups, tile, 0)
    for n in range(len(blocks)):
        for g in range(groups):
            copies(n, g).wait()


def exchange(peers):
    up = [(i, i + 1) for i in range(1, peers - 1, 2)]
    return up, [(j, i) for i, j in up]


def on_device(forward_field, adjoint_field):
    cells, parts, freqs, width = forward_field.shape
    terms, tiles = parts * freqs, width // LANES
    peers = lax.axis_size("gx")
    me = lax.axis_index("gx")
    core = (me % 2).astype(jnp.int32).reshape(1)
    cores = [(i, i + 1) for i in range(0, peers, 2)] + [(i + 1, i) for i in range(0, peers, 2)]
    links = sum(exchange(peers), [])
    row_bytes = 2 * terms * width * 2

    *own, whole = pack(core, forward_field, adjoint_field)
    arrived = []
    for g, sent in enumerate(own):
        if g == 2:
            sent = held(sent, arrived[0][0, 0, 0])
        arrived.append(lax.ppermute(sent, "gx", links))
    beside = lax.ppermute(whole, "gx", cores)

    def layout(count):
        operands = own + [beside]
        where = {}
        order = [i for chunk in CHUNKS for i in chunk]
        for g, chunk in enumerate(CHUNKS):
            where.update({cells - i: (g, k) for k, i in enumerate(chunk)})
        where.update({i - cells - 1: (len(own), k) for k, i in enumerate(order)})
        for chunk, got in zip(CHUNKS[:count], arrived):
            where.update({cells - 1 + i: (len(operands), k) for k, i in enumerate(chunk)})
            operands.append(got)
        return operands, where

    def count(blocks, keep):
        total = 0
        for blk in blocks:
            lags = [blk * BLOCK + t - HALF for t in range(BLOCK)]
            total += sum(len(pairs) for pairs in blocks_of(cells, lags, keep))
        return total

    def cost(pairs, lags):
        return pl.CostEstimate(
            flops=RATE * (2 * pairs * terms * width + 20 * lags * cells * width),
            bytes_accessed=lags * cells * width * 4,
            transcendentals=0,
        )

    groups = tiles // SUB

    def partial(name, pieces_in, blocks, done):
        operands, where = layout(pieces_in)
        pairs = count(
            blocks, lambda a, b: a in where and b in where and not (a in done and b in done)
        )
        out = pl.pallas_call(
            functools.partial(part_kernel, cells, blocks, where, done),
            in_specs=[VMEM] * len(operands),
            out_specs=VMEM,
            out_shape=jax.ShapeDtypeStruct(
                (len(blocks), BLOCK, cells + 2, tiles, LANES), jnp.float32
            ),
            compiler_params=pltpu.CompilerParams(vmem_limit_bytes=SCOPED),
            cost_estimate=cost(pairs if done else 0, 0),
            name=name,
        )(*operands)
        return out, (set(where), blocks)

    operands, where = layout(1)
    lo, hi = pl.pallas_call(
        functools.partial(rim_kernel, cells, where),
        in_specs=[VMEM] * len(operands),
        out_specs=[VMEM, VMEM],
        out_shape=[jax.ShapeDtypeStruct((2, tiles, LANES), jnp.float32)] * 2,
        cost_estimate=pl.CostEstimate(
            flops=0, bytes_accessed=0, transcendentals=0
        ),
        compiler_params=pltpu.CompilerParams(vmem_limit_bytes=SMALL),
        name="rim",
    )(*operands)
    rim_lo = lax.ppermute(lo, "gx", cores)
    rim_hi = lax.ppermute(hi, "gx", links)

    def lags(name, image, pieces_in, blocks, partials, stages, rims):
        operands, where = layout(pieces_in)
        operands = [core] + operands + partials + rims
        specs = [SMEM] + [VMEM] * (len(operands) - 1)
        aliases = {}
        if image is not None:
            aliases = {len(operands): 0}
            operands.append(image)
            specs.append(ANY)
        nblk = len(blocks)
        pairs = count(
            blocks, lambda a, b: not any(a in rows and b in rows for rows, _ in stages)
        )
        return pl.pallas_call(
            functools.partial(
                lag_kernel, cells, blocks, where, stages, bool(rims), image is not None
            ),
            in_specs=specs,
            out_specs=ANY,
            out_shape=jax.ShapeDtypeStruct((LAGS, cells, width), jnp.float32),
            scratch_shapes=[
                pltpu.VMEM((BLOCK, cells + 2, SUB, LANES), jnp.float32),
                pltpu.VMEM((BLOCK, SUB * cells, LANES), jnp.float32),
                pltpu.VMEM((nblk, groups, BLOCK, cells, SUB * LANES), jnp.float32),
                pltpu.SemaphoreType.DMA((nblk, groups)),
            ],
            input_output_aliases=aliases,
            compiler_params=pltpu.CompilerParams(vmem_limit_bytes=SCOPED),
            cost_estimate=cost(pairs, BLOCK * nblk),
            name=name,
        )(*operands)

    inner, first = partial("inner", 1, ALL, ())
    image = lags("near", None, 2, NEAR, [inner], [first], [])
    middle, second = partial("middle", 2, FAR, first[0])
    return lags("far", image, 3, FAR, [inner, middle], [first, second], [rim_lo, rim_hi])


def solution(mesh):
    placed = (P(("shots", "gx"), None, None, None), P(("shots", "gx"), None, None, None))
    return jax.shard_map(
        on_device,
        mesh=mesh,
        in_specs=placed,
        out_specs=P(None, ("shots", "gx"), None),
        check_vma=False,
    )
```
